128 devices in a mesh: dp: 16 (over x, y), seq: 8 (over z, core).
Axes of the slice: x: 4, y: 4, z: 4, core: 2. Of those that a mesh axis runs over, the one named last changes fastest.
Arguments:
- queries: bfloat16 [32, 512, 5120], P('dp', 'seq'), may hold values from -50 to 50
- key_rows: bfloat16 [32, 512, 1024], P('dp', 'seq'), may hold values from -6 to 6
- value_rows: bfloat16 [32, 512, 1024], P('dp', 'seq'), may hold values from -6 to 6
- cotangent: bfloat16 [32, 512, 5120], P('dp', 'seq'), may hold values from -6 to 6
- episodes: int32 [32, 512], P('dp', 'seq'), may hold values from 0 to 7, never falling along the last dimension, each value on 1 to 341 neighbouring positions
- send_slot: int32 [16], P('dp'), may hold values from 0 to 1
- swap_mask: int32 [1], replicated, may hold values from 1 to 15
Outputs:
- grad_queries: bfloat16 [32, 512, 5120], P('dp', 'seq')
- grad_keys: bfloat16 [32, 512, 1024], P('dp', 'seq')
- grad_values: bfloat16 [32, 512, 1024], P('dp', 'seq')
The draws below stay inside these ranges and needn't reach their ends.
Inputs may be any that keep to these rules, and one draw needn't show every extreme that they name: `episodes`: episode ids never fall along a span.
All inputs are finite; a program needn't handle non-finite values.
Results may differ from the reference program's by a relative error of at most 0.0055.
Values may be sent and summed in bfloat16 or wider, within the bound.
No kernel may reach another device: no remote copies, remote signals or barrier semaphores. Data moves between devices by JAX's collectives and lax.ppermute only.
A program may use at most 64 MiB of HBM per device.

```python
import math
import jax
import jax.numpy as jnp
import numpy as np
from jax import lax

H = 40
KVH = 8
DH = 128
SPANS = 2
EPIS = 8
SPAN_LEN = 512
MOST = 341
ALL_SPANS = 32
N_DP = 16


def paired_draw(key):
    first, second = jax.random.split(jax.random.fold_in(key, 17), 2)
    groups = H // KVH
    query_part = jnp.clip(jax.random.normal(first, (ALL_SPANS, SPAN_LEN, KVH, groups, DH), jnp.float32), -6.0, 6.0)
    key_part = jnp.clip(jax.random.normal(second, (ALL_SPANS, SPAN_LEN, KVH, DH), jnp.float32), -6.0, 6.0)
    return (query_part.reshape(ALL_SPANS, SPAN_LEN, H * DH), key_part.reshape(ALL_SPANS, SPAN_LEN, KVH * DH))


def draw_queries(key, part):
    return paired_draw(key)[0].astype(jnp.bfloat16)


def draw_key_rows(key, part):
    return paired_draw(key)[1].astype(jnp.bfloat16)


def set_ends(values, rng, low, top_value):
    longest = values.shape.index(max(values.shape))
    spots = []
    for shift in (0, 1):
        where = [jax.random.randint(jax.random.fold_in(rng, axis), (), 0, length) for axis, length in enumerate(values.shape)]
        where[longest] = (where[longest] + shift) % values.shape[longest]
        spots.append(tuple(where))
    return values.at[spots[0]].set(low).at[spots[1]].set(top_value)


def level_of(key, shape, pieces, least, high):
    def one(dim, shards_of):
        steps = jax.random.uniform(jax.random.fold_in(jax.random.fold_in(key, 6), dim), (shards_of,), jnp.float32, least / len(pieces), high / len(pieces))
        return jnp.repeat(jnp.exp(steps), shape[dim] // shards_of).reshape((-1,) + (1,) * (len(shape) - dim - 1))

    loudness = one(*pieces[0])
    for cut in pieces[1:]:
        loudness = loudness * one(*cut)
    return loudness


def split_up(count, total, limit, slope):
    portions = [(1 << 20) // math.isqrt(standing ** slope) + 1 for standing in range(2, count + 1)]
    surplus, given = total - limit - (count - 1), [1] * (count - 1)
    while surplus > 0:
        movable = [i for i in range(count - 1) if given[i] < limit]
        pool, left = sum([portions[i] for i in movable]), surplus
        for i in movable:
            more = min(limit - given[i], max(1, left * portions[i] // pool), surplus)
            given[i] = given[i] + more
            surplus = surplus - more
    return np.array([limit] + given)


def ragged(rng, count, total, reach, lean):
    if count == 2:
        one = jax.random.randint(rng, (), max(1, total - reach), min(reach, total - 1) + 1)
        return jnp.stack([one, total - one])
    tallies = jnp.asarray(split_up(count, total, reach, lean), jnp.int32)
    couples = (count - 1) // 2
    donor, receiver = tallies[1:1 + 2 * couples:2], tallies[2:2 + 2 * couples:2]
    room = jnp.minimum(donor - 1, reach - receiver)
    moved = jax.random.randint(jax.random.fold_in(rng, 1), (couples,), 0, 1 << 20) % (room + 1)
    tallies = tallies.at[1:1 + 2 * couples:2].set(donor - moved).at[2:2 + 2 * couples:2].set(receiver + moved)
    return tallies[jax.random.permutation(jax.random.fold_in(rng, 2), count)]


def bell_draw(own_key, extent, deviation, bound, pieces=(), held_as=jnp.bfloat16):
    loudness = level_of(own_key, extent, pieces, -0.22, 0.18) if pieces else 1.0
    values = jax.random.normal(own_key, extent, jnp.float32) * deviation * loudness
    return jnp.minimum(jnp.maximum(values, -bound), bound).astype(held_as)


def setup_inputs(seed: int = 0) -> dict:
    key_list = jax.random.split(jax.random.key(seed), 8)
    return {
        "queries": draw_queries(jax.random.fold_in(key_list[7], 71), 0),
        "key_rows": draw_key_rows(jax.random.fold_in(key_list[7], 71), 0),
        "value_rows": bell_draw(key_list[2], (ALL_SPANS, SPAN_LEN, KVH * DH), 1.0, 6.0, ((0, 16), (1, 8))),
        "cotangent": bell_draw(key_list[3], (ALL_SPANS, SPAN_LEN, H * DH), 1.0, 6.0, ((0, 16), (1, 8))),
        "episodes": jax.vmap(lambda own: jnp.searchsorted(jnp.cumsum(ragged(own, EPIS, SPAN_LEN, MOST, 2)), jnp.arange(SPAN_LEN), side="right"))(jax.random.split(key_list[4], ALL_SPANS)).reshape((ALL_SPANS, SPAN_LEN)).astype(jnp.int32),
        "send_slot": set_ends(jax.random.randint(key_list[5], (N_DP,), 0, 2), jax.random.fold_in(key_list[5], 1), 0, 1).astype(jnp.int32),
        "swap_mask": jax.random.randint(key_list[6], (1,), 1, N_DP).astype(jnp.int32),
    }


def head_group(query_group, key_head, value_head, grad_group, episode_ids):
    scaling = 1.0 / jnp.sqrt(jnp.float32(DH))
    query_full = query_group.astype(jnp.float32)
    key_full = key_head.astype(jnp.float32)
    value_full = value_head.astype(jnp.float32)
    grad_full = grad_group.astype(jnp.float32)
    scores = jnp.einsum('qgd,td->gqt', query_full, key_full) * scaling
    positions = jnp.arange(SPAN_LEN, dtype=jnp.int32)
    allowed = (episode_ids[:, None] == episode_ids[None, :]) & (positions[:, None] >= positions[None, :])
    scores = jnp.where(allowed[None], scores, jnp.float32(-1e+30))
    top = lax.optimization_barrier(jnp.max(scores, axis=-1, keepdims=True))
    expo = jnp.exp(scores - top)
    probs = expo / lax.optimization_barrier(jnp.sum(expo, axis=-1, keepdims=True))
    probs_low = lax.optimization_barrier(probs.astype(jnp.bfloat16)).astype(jnp.float32)
    dprobs = jnp.einsum('qgd,td->gqt', grad_full, value_full)
    delta = lax.optimization_barrier(jnp.sum(probs * dprobs, axis=-1, keepdims=True))
    dscores = lax.optimization_barrier((probs * (dprobs - delta)).astype(jnp.bfloat16)).astype(jnp.float32)
    grad_value = jnp.einsum('gqt,qgd->td', probs_low, grad_full).astype(jnp.bfloat16)
    grad_query = (jnp.einsum('gqt,td->qgd', dscores, key_full) * scaling).astype(jnp.bfloat16)
    grad_key = (jnp.einsum('gqt,qgd->td', dscores, query_full) * scaling).astype(jnp.bfloat16)
    return (grad_query, grad_key, grad_value)

def span_grads(packed):
    query_span, key_span, value_span, grad_span, episode_ids = packed
    groups = H // KVH
    query_heads = query_span.reshape(SPAN_LEN, KVH, groups, DH).transpose(1, 0, 2, 3)
    grad_heads = grad_span.reshape(SPAN_LEN, KVH, groups, DH).transpose(1, 0, 2, 3)
    key_heads = key_span.reshape(SPAN_LEN, KVH, DH).transpose(1, 0, 2)
    value_heads = value_span.reshape(SPAN_LEN, KVH, DH).transpose(1, 0, 2)

    def per_head(packed_group):
        return head_group(packed_group[0], packed_group[1], packed_group[2], packed_group[3], episode_ids)
    grad_query, grad_key, grad_value = lax.map(per_head, (query_heads, key_heads, value_heads, grad_heads))
    grad_query = grad_query.transpose(1, 0, 2, 3).reshape(SPAN_LEN, H * DH)
    grad_key = grad_key.transpose(1, 0, 2).reshape(SPAN_LEN, KVH * DH)
    grad_value = grad_value.transpose(1, 0, 2).reshape(SPAN_LEN, KVH * DH)
    return (grad_query, grad_key, grad_value)

def reference(queries, key_rows, value_rows, cotangent, episodes, send_slot, swap_mask):
    grad_query, grad_key, grad_value = lax.map(span_grads, (queries, key_rows, value_rows, cotangent, episodes))
    replicas = jnp.arange(N_DP, dtype=jnp.int32)
    partner = jnp.bitwise_xor(replicas, swap_mask[0]).astype(jnp.int32)
    kept_index = replicas * SPANS + 1 - send_slot
    taken_index = partner * SPANS + send_slot[partner]
    order = jnp.stack([kept_index, taken_index], axis=1).reshape(-1).astype(jnp.int32)
    return (grad_query[order], grad_key[order], grad_value[order])
```

```python
import functools
import math

import jax
import jax.numpy as jnp
from jax import lax
from jax.experimental import pallas as pl
from jax.experimental.pallas import tpu as pltpu
from jax.sharding import PartitionSpec as P

H = 40
KVH = 8
DH = 128
GROUPS = H // KVH
LOCAL_KV = KVH // 2
CHIPS = 4
TOK = 64
CHUNK = 2 * TOK
KEYS = CHIPS * CHUNK
QW = H * DH // 2
KW = LOCAL_KV * DH
KVW = 2 * KW
ROWS_Q = GROUPS * CHUNK
SCALE = 1.0 / math.sqrt(DH)
SCALE2 = SCALE * math.log2(math.e)
BF = jnp.bfloat16
F32 = jnp.float32
VMEM_LIMIT = 40 * 1024 * 1024


def interleave(out, rows, k, v):
    for g in range(LOCAL_KV):
        out[rows, 2 * g * DH : (2 * g + 1) * DH] = k[:, g * DH : (g + 1) * DH]
        out[rows, (2 * g + 1) * DH : (2 * g + 2) * DH] = v[:, g * DH : (g + 1) * DH]


def pack_kv_kernel(where, k, v, ids, out):
    i = pl.program_id(0)
    interleave(out.at[0], slice(0, TOK), k.at[0], v.at[0])
    e = jnp.where(where[2 + i] == 0, ids[0:1, :], ids[1:2, :])
    out[0, TOK : TOK + 16, 0:DH] = jnp.broadcast_to(e.astype(F32), (16, DH)).astype(BF)


def pack_kv(where, key_rows, value_rows, ids):
    column = lambda i, w: (w[2 + i], 0, 1 - w[1])
    return pl.pallas_call(
        pack_kv_kernel,
        grid_spec=pltpu.PrefetchScalarGridSpec(
            num_scalar_prefetch=1,
            grid=(2,),
            in_specs=[
                pl.BlockSpec((1, TOK, KW), column),
                pl.BlockSpec((1, TOK, KW), column),
                pl.BlockSpec((2, DH), lambda i, w: (0, 0)),
            ],
            out_specs=pl.BlockSpec((1, TOK + 16, KVW), lambda i, w: (i, 0, 0)),
        ),
        out_shape=jax.ShapeDtypeStruct((2, TOK + 16, KVW), BF),
        cost_estimate=pl.CostEstimate(flops=0, bytes_accessed=1 << 20, transcendentals=0),
        name="pack_kv",
    )(where, key_rows, value_rows, ids)


def pack_q_kernel(where, q, c, out):
    out[0, 0] = q[0]
    out[0, 1] = c[0]


def pack_q(where, queries, cotangent):
    column = lambda i, w: (w[2 + i], 0, 1 - w[1])
    return pl.pallas_call(
        pack_q_kernel,
        grid_spec=pltpu.PrefetchScalarGridSpec(
            num_scalar_prefetch=1,
            grid=(2,),
            in_specs=[pl.BlockSpec((1, TOK, QW), column)] * 2,
            out_specs=pl.BlockSpec((1, 2, TOK, QW), lambda i, w: (i, 0, 0, 0)),
        ),
        out_shape=jax.ShapeDtypeStruct((2, 2, TOK, QW), BF),
        cost_estimate=pl.CostEstimate(flops=0, bytes_accessed=3 << 20, transcendentals=0),
        name="pack_q",
    )(where, queries, cotangent)


def chunks_kernel(where, kh, vh, kk, vk, ids, got, out_h, out_k):
    interleave(out_h, slice(0, TOK), kh.at[0], vh.at[0])
    out_h[TOK:CHUNK, :] = got[0, :TOK, :]
    interleave(out_k, slice(0, TOK), kk.at[0], vk.at[0])
    out_k[TOK:CHUNK, :] = got[1, :TOK, :]
    first = lax.broadcasted_iota(jnp.int32, (16, DH), 1) < TOK
    for i in range(2):
        e = jnp.where(where[2 + i] == 0, ids[0:1, :], ids[1:2, :])
        mine = jnp.broadcast_to(e.astype(F32), (16, DH))
        theirs = got[i, TOK : TOK + 16, 0:DH].astype(F32)
        out_h[CHUNK : CHUNK + 16, i * DH : (i + 1) * DH] = jnp.where(first, mine, theirs).astype(BF)


def make_chunks(where, key_rows, value_rows, ids, got):
    def own(i):
        return pl.BlockSpec((1, TOK, KW), lambda _, w: (w[2 + i], 0, w[1]))

    return pl.pallas_call(
        chunks_kernel,
        grid_spec=pltpu.PrefetchScalarGridSpec(
            num_scalar_prefetch=1,
            grid=(1,),
            in_specs=[
                own(0),
                own(0),
                own(1),
                own(1),
                pl.BlockSpec((2, DH), lambda i, w: (0, 0)),
                pl.BlockSpec((2, TOK + 16, KVW), lambda i, w: (0, 0, 0)),
            ],
            out_specs=[
                pl.BlockSpec((CHUNK + 16, KVW), lambda i, w: (0, 0)),
                pl.BlockSpec((CHUNK, KVW), lambda i, w: (0, 0)),
            ],
        ),
        out_shape=[
            jax.ShapeDtypeStruct((CHUNK + 16, KVW), BF),
            jax.ShapeDtypeStruct((CHUNK, KVW), BF),
        ],
        cost_estimate=pl.CostEstimate(flops=0, bytes_accessed=2 << 20, transcendentals=0),
        name="make_chunks",
    )(where, key_rows, value_rows, key_rows, value_rows, ids, got)


def attention_kernel(
    where, qo, co, qx, k0, k1, k2, k3, i0, i1, i2, i3,
    gqo, gqx, p0, p1, p2, p3, bias, st, dt, pt, ds,
):
    chip = where[0]
    core = where[1]

    @pl.when(pl.program_id(0) == 0)
    def _():
        rows = lax.broadcasted_iota(jnp.int32, (CHUNK, CHUNK), 0)
        lanes = lax.broadcasted_iota(jnp.int32, (CHUNK, CHUNK), 1)
        query_pos = chip * CHUNK + ((lanes + core * TOK) & (CHUNK - 1))
        query_id = jnp.broadcast_to(i0[0:1, :].astype(F32), (CHUNK, CHUNK))
        for d, ids in enumerate((i0, i1, i2, i3)):
            key_pos = ((chip - d) & (CHIPS - 1)) * CHUNK + ((rows + core * TOK) & (CHUNK - 1))
            key_id = jnp.broadcast_to(ids[0:1, :].astype(F32), (CHUNK, CHUNK)).T
            allowed = (key_id == query_id) & (key_pos <= query_pos)
            bias[d * CHUNK : (d + 1) * CHUNK, :] = jnp.where(allowed, 0.0, -1e30).astype(F32)

    kv = [k[0:CHUNK, :] for k in (k0, k1, k2, k3)]
    keys = jnp.concatenate([x[:, :DH] for x in kv], axis=0)
    values = jnp.concatenate([x[:, DH:] for x in kv], axis=0)

    def heads(own, other):
        parts = []
        for h in range(GROUPS):
            parts.append(own[:, h * DH : (h + 1) * DH])
            parts.append(other[:, h * DH : (h + 1) * DH])
        return jnp.concatenate(parts, axis=0)

    queries = heads(qo[0], qx[0, 0])
    cots = heads(co[0], qx[0, 1])
    last = (((1,), (1,)), ((), ()))
    st[...] = lax.dot_general(keys, queries, last, preferred_element_type=F32)
    dt[...] = lax.dot_general(values, cots, last, preferred_element_type=F32)
    for h in range(GROUPS):
        cut = slice(h * CHUNK, (h + 1) * CHUNK)
        s = st[:, cut] * SCALE2 + bias[...]
        top = jnp.max(s, axis=0, keepdims=True)
        e = jnp.exp2(s - top)
        probs = e * (1.0 / jnp.sum(e, axis=0, keepdims=True))
        dprobs = dt[:, cut]
        delta = jnp.sum(probs * dprobs, axis=0, keepdims=True)
        pt[:, cut] = probs.astype(BF)
        ds[:, cut] = (probs * (dprobs - delta)).astype(BF)
    grad_k = jnp.dot(ds[...], queries, preferred_element_type=F32) * SCALE
    grad_v = jnp.dot(pt[...], cots, preferred_element_type=F32)
    for d, p in enumerate((p0, p1, p2, p3)):
        cut = slice(d * CHUNK, (d + 1) * CHUNK)
        p[:, :DH] = grad_k[cut].astype(p.dtype)
        p[:, DH:] = grad_v[cut].astype(p.dtype)
    gq_t = jnp.dot(keys.T, ds[...], preferred_element_type=F32) * SCALE
    for h in range(GROUPS):
        gq = gq_t[:, h * CHUNK : (h + 1) * CHUNK].T.astype(BF)
        gqo[:, h * DH : (h + 1) * DH] = gq[:TOK]
        gqx[:, h * DH : (h + 1) * DH] = gq[TOK:]


def attention(where, which, queries, cotangent, q_other, chunks, id_chunks):
    own = pl.BlockSpec((1, TOK, GROUPS * DH), lambda g, w: (w[2 + which], 0, w[1] * LOCAL_KV + g))
    other = pl.BlockSpec((1, 2, TOK, GROUPS * DH), lambda g, w: (which, 0, 0, g))
    chunk = pl.BlockSpec((CHUNK, 2 * DH), lambda g, w: (0, g))
    ids = pl.BlockSpec((16, DH), lambda g, w: (CHUNK // 16, which))
    out_q = pl.BlockSpec((TOK, GROUPS * DH), lambda g, w: (0, g))
    return pl.pallas_call(
        attention_kernel,
        grid_spec=pltpu.PrefetchScalarGridSpec(
            num_scalar_prefetch=1,
            grid=(LOCAL_KV,),
            in_specs=[own, own, other] + [chunk] * 4 + [ids] * 4,
            out_specs=[out_q, out_q] + [chunk] * 4,
            scratch_shapes=[
                pltpu.VMEM((KEYS, CHUNK), F32),
                pltpu.VMEM((KEYS, ROWS_Q), F32),
                pltpu.VMEM((KEYS, ROWS_Q), F32),
                pltpu.VMEM((KEYS, ROWS_Q), BF),
                pltpu.VMEM((KEYS, ROWS_Q), BF),
            ],
        ),
        out_shape=[jax.ShapeDtypeStruct((TOK, QW), BF)] * 2
        + [jax.ShapeDtypeStruct((CHUNK, KVW), F32)]
        + [jax.ShapeDtypeStruct((CHUNK, KVW), BF)] * 3,
        compiler_params=pltpu.CompilerParams(
            dimension_semantics=("arbitrary",), vmem_limit_bytes=VMEM_LIMIT
        ),
        cost_estimate=pl.CostEstimate(
            flops=10 * KEYS * ROWS_Q * DH * LOCAL_KV,
            bytes_accessed=5 << 20,
            transcendentals=KEYS * ROWS_Q * LOCAL_KV,
        ),
        name="attention",
    )(where, queries, cotangent, q_other, *chunks, *id_chunks)


def total_kernel(p0, r1, r2, r3, own, other):
    total = (p0[...] + r1[...].astype(F32)) + (r2[...].astype(F32) + r3[...].astype(F32))
    total = total.astype(BF)
    own[...] = total[:TOK]
    other[...] = total[TOK:]


def total_kv(parts):
    return pl.pallas_call(
        total_kernel,
        out_shape=[jax.ShapeDtypeStruct((TOK, KVW), BF)] * 2,
        cost_estimate=pl.CostEstimate(flops=0, bytes_accessed=2 << 20, transcendentals=0),
        name="total_kv",
    )(*parts)


def place_q_kernel(where, kept_own, kept_other, new_own, new_other, out):
    for core in range(2):

        @pl.when(where[1] == core)
        def _():
            a = slice(core * QW, (core + 1) * QW)
            b = slice((1 - core) * QW, (2 - core) * QW)
            out[0, :, a] = kept_own[...]
            out[0, :, b] = kept_other[...]
            out[1, :, a] = new_own[...]
            out[1, :, b] = new_other[...]


def place_q(where, *parts):
    return pl.pallas_call(
        place_q_kernel,
        grid_spec=pltpu.PrefetchScalarGridSpec(
            num_scalar_prefetch=1,
            grid=(1,),
            in_specs=[pl.BlockSpec((TOK, QW), lambda i, w: (0, 0))] * 4,
            out_specs=pl.BlockSpec((2, TOK, 2 * QW), lambda i, w: (0, 0, 0)),
        ),
        out_shape=jax.ShapeDtypeStruct((2, TOK, 2 * QW), BF),
        cost_estimate=pl.CostEstimate(flops=0, bytes_accessed=3 << 20, transcendentals=0),
        name="place_q",
    )(where, *parts)


def place_kv_kernel(where, kept_own, kept_other, new_own, new_other, out_k, out_v):
    for core in range(2):

        @pl.when(where[1] == core)
        def _():
            for slot, at, part in (
                (0, core, kept_own),
                (0, 1 - core, kept_other),
                (1, core, new_own),
                (1, 1 - core, new_other),
            ):
                for g in range(LOCAL_KV):
                    to = slice(at * KW + g * DH, at * KW + (g + 1) * DH)
                    out_k[slot, :, to] = part[:, 2 * g * DH : (2 * g + 1) * DH]
                    out_v[slot, :, to] = part[:, (2 * g + 1) * DH : (2 * g + 2) * DH]


def place_kv(where, *parts):
    return pl.pallas_call(
        place_kv_kernel,
        grid_spec=pltpu.PrefetchScalarGridSpec(
            num_scalar_prefetch=1,
            grid=(1,),
            in_specs=[pl.BlockSpec((TOK, KVW), lambda i, w: (0, 0))] * 4,
            out_specs=[pl.BlockSpec((2, TOK, 2 * KW), lambda i, w: (0, 0, 0))] * 2,
        ),
        out_shape=[jax.ShapeDtypeStruct((2, TOK, 2 * KW), BF)] * 2,
        cost_estimate=pl.CostEstimate(flops=0, bytes_accessed=2 << 20, transcendentals=0),
        name="place_kv",
    )(where, *parts)


def core_swap(x):
    return lax.ppermute(x, "seq", [(i, i ^ 1) for i in range(2 * CHIPS)])


def up(x, d):
    pairs = [(2 * z + c, 2 * (z + d) + c) for z in range(CHIPS - d) for c in range(2)]
    return lax.ppermute(x, "seq", pairs)


def down(x, d):
    pairs = [(2 * (z + d) + c, 2 * z + c) for z in range(CHIPS - d) for c in range(2)]
    return lax.ppermute(x, "seq", pairs)


def trade(x, replicas, mask, cross):
    n = 2 * CHIPS
    pairs = [(r * n + s, (r ^ mask) * n + (s ^ cross)) for r in range(replicas) for s in range(n)]
    return lax.ppermute(x, ("dp", "seq"), pairs)


def gradients(mask, replicas, where, ids, queries, key_rows, value_rows, cotangent):
    got = core_swap(pack_kv(where, key_rows, value_rows, ids))
    q_other = core_swap(pack_q(where, queries, cotangent))
    chunk_h, chunk_k = make_chunks(where, key_rows, value_rows, ids, got)
    chunks_h = [chunk_h] + [up(chunk_h, d) for d in range(1, CHIPS)]
    chunks_k = [chunk_k] + [up(chunk_k, d) for d in range(1, CHIPS)]
    swap = functools.partial(trade, replicas=replicas, mask=mask)

    gq_own, gq_other, *parts = attention(
        where, 0, queries, cotangent, q_other, chunks_h, chunks_h
    )
    new_own, new_other = swap(gq_own, cross=0), swap(gq_other, cross=1)
    sums_h = [parts[0]] + [down(parts[d], d) for d in range(1, CHIPS)]
    kept_own, kept_other, *parts = attention(
        where, 1, queries, cotangent, q_other, chunks_k, chunks_h
    )
    kept_other = core_swap(kept_other)
    sums_k = [parts[0]] + [down(parts[d], d) for d in range(1, CHIPS)]
    own, other = total_kv(sums_h)
    kv_new_own, kv_new_other = swap(own, cross=0), swap(other, cross=1)
    own, other = total_kv(sums_k)
    grad_queries = place_q(where, kept_own, kept_other, new_own, new_other)
    grad_keys, grad_values = place_kv(where, own, core_swap(other), kv_new_own, kv_new_other)
    return grad_queries, grad_keys, grad_values


def per_device(queries, key_rows, value_rows, cotangent, episodes, send_slot, swap_mask):
    replicas = lax.axis_size("dp")
    s = lax.axis_index("seq")
    handed = send_slot[0]
    where = jnp.stack([s // 2, s % 2, handed, 1 - handed]).astype(jnp.int32)
    ids = jnp.concatenate([episodes, episodes], axis=1)
    branches = [functools.partial(gradients, m, replicas) for m in range(1, replicas)]
    return lax.switch(
        swap_mask[0] - 1, branches, where, ids, queries, key_rows, value_rows, cotangent
    )


def solution(mesh):
    spec = P("dp", "seq", None)
    return jax.shard_map(
        per_device,
        mesh=mesh,
        in_specs=(spec, spec, spec, spec, P("dp", "seq"), P("dp"), P()),
        out_specs=(spec, spec, spec),
        check_vma=False,
    )
```

```python
import functools
import math

import jax
import jax.numpy as jnp
from jax import lax
from jax.experimental import pallas as pl
from jax.experimental.pallas import tpu as pltpu
from jax.sharding import PartitionSpec as P

H = 40
KVH = 8
DH = 128
GROUPS = H // KVH
LOCAL_KV = KVH // 2
CHIPS = 4
TOK = 64
CHUNK = 2 * TOK
KEYS = CHIPS * CHUNK
QW = H * DH // 2
KW = LOCAL_KV * DH
KVW = 2 * KW
ROWS_Q = GROUPS * CHUNK
SCALE = 1.0 / math.sqrt(DH)
SCALE2 = SCALE * math.log2(math.e)
BF = jnp.bfloat16
F32 = jnp.float32
VMEM_LIMIT = 16 * 1024 * 1024
SMALL_LIMIT = 8 * 1024 * 1024


def interleave(out, rows, k, v):
    for g in range(LOCAL_KV):
        out[rows, 2 * g * DH : (2 * g + 1) * DH] = k[:, g * DH : (g + 1) * DH]
        out[rows, (2 * g + 1) * DH : (2 * g + 2) * DH] = v[:, g * DH : (g + 1) * DH]


def core_of(pos):
    return pos[0] & 1


def span_of(slot, i):
    return slot[0] ^ i


def id_tile(ids, slot, i):
    e = jnp.where(span_of(slot, i) == 0, ids[0:1, :], ids[1:2, :]).astype(F32)
    return jnp.broadcast_to(jnp.concatenate([e, e], axis=1), (16, DH))


def pack_kv_kernel(pos, slot, k, v, ids, out):
    for i in range(2):
        span = span_of(slot, i)
        interleave(out.at[i], slice(0, TOK), k.at[span], v.at[span])
        out[i, TOK : TOK + 16, 0:DH] = id_tile(ids, slot, i).astype(BF)


def pack_kv(where, key_rows, value_rows, episodes):
    return pl.pallas_call(
        pack_kv_kernel,
        grid_spec=pltpu.PrefetchScalarGridSpec(
            num_scalar_prefetch=2,
            grid=(1,),
            in_specs=[
                pl.BlockSpec((2, TOK, KW), lambda i, p, s: (0, 0, 1 - core_of(p))),
                pl.BlockSpec((2, TOK, KW), lambda i, p, s: (0, 0, 1 - core_of(p))),
                pl.BlockSpec((2, TOK), lambda i, p, s: (0, 0)),
            ],
            out_specs=pl.BlockSpec((2, TOK + 16, KVW), lambda i, p, s: (0, 0, 0)),
        ),
        out_shape=jax.ShapeDtypeStruct((2, TOK + 16, KVW), BF),
        cost_estimate=pl.CostEstimate(flops=0, bytes_accessed=1 << 20, transcendentals=0),
        compiler_params=pltpu.CompilerParams(vmem_limit_bytes=SMALL_LIMIT),
        name="pack_kv",
    )(*where, key_rows, value_rows, episodes)


def pack_q_kernel(pos, slot, q, c, out):
    out[0, 0] = q[0]
    out[0, 1] = c[0]


def pack_q(where, queries, cotangent):
    column = lambda i, p, s: (span_of(s, i), 0, 1 - core_of(p))
    return pl.pallas_call(
        pack_q_kernel,
        grid_spec=pltpu.PrefetchScalarGridSpec(
            num_scalar_prefetch=2,
            grid=(2,),
            in_specs=[pl.BlockSpec((1, TOK, QW), column)] * 2,
            out_specs=pl.BlockSpec((1, 2, TOK, QW), lambda i, p, s: (i, 0, 0, 0)),
        ),
        out_shape=jax.ShapeDtypeStruct((2, 2, TOK, QW), BF),
        cost_estimate=pl.CostEstimate(flops=0, bytes_accessed=3 << 20, transcendentals=0),
        compiler_params=pltpu.CompilerParams(vmem_limit_bytes=SMALL_LIMIT),
        name="pack_q",
    )(*where, queries, cotangent)


def chunks_kernel(pos, slot, k, v, ids, got, out_h, out_k):
    first = lax.broadcasted_iota(jnp.int32, (16, DH), 1) < TOK
    for i, out in enumerate((out_h, out_k)):
        span = span_of(slot, i)
        interleave(out, slice(0, TOK), k.at[span], v.at[span])
        out[TOK:CHUNK, :] = got[i, :TOK, :]
        theirs = got[i, TOK : TOK + 16, 0:DH].astype(F32)
        both = jnp.where(first, id_tile(ids, slot, i), theirs).astype(BF)
        out_h[CHUNK : CHUNK + 16, i * DH : (i + 1) * DH] = both


def make_chunks(where, key_rows, value_rows, episodes, got):
    own = pl.BlockSpec((2, TOK, KW), lambda i, p, s: (0, 0, core_of(p)))
    return pl.pallas_call(
        chunks_kernel,
        grid_spec=pltpu.PrefetchScalarGridSpec(
            num_scalar_prefetch=2,
            grid=(1,),
            in_specs=[
                own,
                own,
                pl.BlockSpec((2, TOK), lambda i, p, s: (0, 0)),
                pl.BlockSpec((2, TOK + 16, KVW), lambda i, p, s: (0, 0, 0)),
            ],
            out_specs=[
                pl.BlockSpec((CHUNK + 16, KVW), lambda i, p, s: (0, 0)),
                pl.BlockSpec((CHUNK, KVW), lambda i, p, s: (0, 0)),
            ],
        ),
        out_shape=[
            jax.ShapeDtypeStruct((CHUNK + 16, KVW), BF),
            jax.ShapeDtypeStruct((CHUNK, KVW), BF),
        ],
        cost_estimate=pl.CostEstimate(flops=0, bytes_accessed=2 << 20, transcendentals=0),
        compiler_params=pltpu.CompilerParams(vmem_limit_bytes=SMALL_LIMIT),
        name="make_chunks",
    )(*where, key_rows, value_rows, episodes, got)


def attention_kernel(
    pos, slot, qo, co, qx, k0, k1, k2, k3, i0, i1, i2, i3,
    gqo, gqx, p0, p1, p2, p3, bias, st, dt, pt, ds,
):
    chip = pos[0] >> 1
    core = core_of(pos)

    @pl.when(pl.program_id(0) == 0)
    def _():
        rows = lax.broadcasted_iota(jnp.int32, (CHUNK, CHUNK), 0)
        lanes = lax.broadcasted_iota(jnp.int32, (CHUNK, CHUNK), 1)
        query_pos = chip * CHUNK + ((lanes + core * TOK) & (CHUNK - 1))
        query_id = jnp.broadcast_to(i0[0:1, :].astype(F32), (CHUNK, CHUNK))
        for d, ids in enumerate((i0, i1, i2, i3)):
            key_pos = ((chip - d) & (CHIPS - 1)) * CHUNK + ((rows + core * TOK) & (CHUNK - 1))
            key_id = jnp.broadcast_to(ids[0:1, :].astype(F32), (CHUNK, CHUNK)).T
            allowed = (key_id == query_id) & (key_pos <= query_pos)
            bias[d * CHUNK : (d + 1) * CHUNK, :] = jnp.where(allowed, 0.0, -1e30).astype(F32)

    kv = [k[0:CHUNK, :] for k in (k0, k1, k2, k3)]
    keys = jnp.concatenate([x[:, :DH] for x in kv], axis=0)
    values = jnp.concatenate([x[:, DH:] for x in kv], axis=0)

    def heads(own, other):
        parts = []
        for h in range(GROUPS):
            parts.append(own[:, h * DH : (h + 1) * DH])
            parts.append(other[:, h * DH : (h + 1) * DH])
        return jnp.concatenate(parts, axis=0)

    queries = heads(qo[0], qx[0, 0])
    cots = heads(co[0], qx[0, 1])
    last = (((1,), (1,)), ((), ()))
    st[...] = lax.dot_general(keys, queries, last, preferred_element_type=F32)
    dt[...] = lax.dot_general(values, cots, last, preferred_element_type=F32)
    for h in range(GROUPS):
        cut = slice(h * CHUNK, (h + 1) * CHUNK)
        s = st[:, cut] * SCALE2 + bias[...]
        top = jnp.max(s, axis=0, keepdims=True)
        e = jnp.exp2(s - top)
        probs = e * (1.0 / jnp.sum(e, axis=0, keepdims=True))
        dprobs = dt[:, cut]
        delta = jnp.sum(probs * dprobs, axis=0, keepdims=True)
        pt[:, cut] = probs.astype(BF)
        ds[:, cut] = (probs * (dprobs - delta)).astype(BF)
    grad_k = jnp.dot(ds[...], queries, preferred_element_type=F32) * SCALE
    grad_v = jnp.dot(pt[...], cots, preferred_element_type=F32)
    for d, p in enumerate((p0, p1, p2, p3)):
        cut = slice(d * CHUNK, (d + 1) * CHUNK)
        p[:, :DH] = grad_k[cut].astype(p.dtype)
        p[:, DH:] = grad_v[cut].astype(p.dtype)
    gq_t = jnp.dot(keys.T, ds[...], preferred_element_type=F32) * SCALE
    for h in range(GROUPS):
        gq = gq_t[:, h * CHUNK : (h + 1) * CHUNK].T.astype(BF)
        gqo[:, h * DH : (h + 1) * DH] = gq[:TOK]
        gqx[:, h * DH : (h + 1) * DH] = gq[TOK:]


def attention(where, which, queries, cotangent, q_other, chunks, id_chunks):
    own = pl.BlockSpec((1, TOK, GROUPS * DH), lambda g, p, s: (span_of(s, which), 0, core_of(p) * LOCAL_KV + g))
    other = pl.BlockSpec((1, 2, TOK, GROUPS * DH), lambda g, p, s: (which, 0, 0, g))
    chunk = pl.BlockSpec((CHUNK, 2 * DH), lambda g, p, s: (0, g))
    ids = pl.BlockSpec((16, DH), lambda g, p, s: (CHUNK // 16, which))
    out_q = pl.BlockSpec((TOK, GROUPS * DH), lambda g, p, s: (0, g))
    return pl.pallas_call(
        attention_kernel,
        grid_spec=pltpu.PrefetchScalarGridSpec(
            num_scalar_prefetch=2,
            grid=(LOCAL_KV,),
            in_specs=[own, own, other] + [chunk] * 4 + [ids] * 4,
            out_specs=[out_q, out_q] + [chunk] * 4,
            scratch_shapes=[
                pltpu.VMEM((KEYS, CHUNK), F32),
                pltpu.VMEM((KEYS, ROWS_Q), F32),
                pltpu.VMEM((KEYS, ROWS_Q), F32),
                pltpu.VMEM((KEYS, ROWS_Q), BF),
                pltpu.VMEM((KEYS, ROWS_Q), BF),
            ],
        ),
        out_shape=[jax.ShapeDtypeStruct((TOK, QW), BF)] * 2
        + [jax.ShapeDtypeStruct((CHUNK, KVW), F32)]
        + [jax.ShapeDtypeStruct((CHUNK, KVW), BF)] * 3,
        compiler_params=pltpu.CompilerParams(
            dimension_semantics=("arbitrary",), vmem_limit_bytes=VMEM_LIMIT
        ),
        cost_estimate=pl.CostEstimate(
            flops=10 * KEYS * ROWS_Q * DH * LOCAL_KV,
            bytes_accessed=5 << 20,
            transcendentals=KEYS * ROWS_Q * LOCAL_KV,
        ),
        name="attention",
    )(*where, queries, cotangent, q_other, *chunks, *id_chunks)


def total_of(p0, r1, r2, r3):
    total = (p0[...] + r1[...].astype(F32)) + (r2[...].astype(F32) + r3[...].astype(F32))
    return total.astype(BF)


def hand_over_kernel(p0, r1, r2, r3, gq_own, gq_got, out):
    total = total_of(p0, r1, r2, r3)
    out[:, 0:QW] = gq_own[...]
    out[:, QW : 2 * QW] = gq_got[...]
    out[:, 2 * QW : 2 * QW + KVW] = total[:TOK]
    out[:, 2 * QW + KVW :] = total[TOK:]


def hand_over(parts, gq_own, gq_got):
    return pl.pallas_call(
        hand_over_kernel,
        out_shape=jax.ShapeDtypeStruct((TOK, 2 * QW + 2 * KVW), BF),
        compiler_params=pltpu.CompilerParams(vmem_limit_bytes=SMALL_LIMIT),
        cost_estimate=pl.CostEstimate(flops=0, bytes_accessed=4 << 20, transcendentals=0),
        name="hand_over",
    )(*parts, gq_own, gq_got)


def keep_kernel(p0, r1, r2, r3, new, own, swap):
    total = total_of(p0, r1, r2, r3)
    own[...] = total[:TOK]
    swap[:, :KVW] = total[TOK:]
    swap[:, KVW:] = new[...]


def keep(parts, new):
    whole = lambda shape: pl.BlockSpec(shape, lambda i: (0, 0))
    return pl.pallas_call(
        keep_kernel,
        grid=(1,),
        in_specs=[whole((CHUNK, KVW))] * 4
        + [pl.BlockSpec((TOK, KVW), lambda i: (0, 2 * QW // KVW + 1))],
        out_specs=[whole((TOK, KVW)), whole((TOK, 2 * KVW))],
        out_shape=[
            jax.ShapeDtypeStruct((TOK, KVW), BF),
            jax.ShapeDtypeStruct((TOK, 2 * KVW), BF),
        ],
        compiler_params=pltpu.CompilerParams(vmem_limit_bytes=SMALL_LIMIT),
        cost_estimate=pl.CostEstimate(flops=0, bytes_accessed=2 << 20, transcendentals=0),
        name="keep",
    )(*parts, new)


def place_q_kernel(pos, slot, kept_own, kept_other, new, out):
    for core in range(2):

        @pl.when(core_of(pos) == core)
        def _():
            a = slice(core * QW, (core + 1) * QW)
            b = slice((1 - core) * QW, (2 - core) * QW)
            out[0, :, a] = kept_own[...]
            out[0, :, b] = kept_other[...]
            out[1, :, a] = new[:, :QW]
            out[1, :, b] = new[:, QW:]


def place_q(where, kept_own, kept_other, new):
    return pl.pallas_call(
        place_q_kernel,
        grid_spec=pltpu.PrefetchScalarGridSpec(
            num_scalar_prefetch=2,
            grid=(1,),
            in_specs=[pl.BlockSpec((TOK, QW), lambda i, p, s: (0, 0))] * 2
            + [pl.BlockSpec((TOK, 2 * QW), lambda i, p, s: (0, 0))],
            out_specs=pl.BlockSpec((2, TOK, 2 * QW), lambda i, p, s: (0, 0, 0)),
        ),
        out_shape=jax.ShapeDtypeStruct((2, TOK, 2 * QW), BF),
        cost_estimate=pl.CostEstimate(flops=0, bytes_accessed=3 << 20, transcendentals=0),
        compiler_params=pltpu.CompilerParams(vmem_limit_bytes=SMALL_LIMIT),
        name="place_q",
    )(*where, kept_own, kept_other, new)


def place_kv_kernel(pos, slot, kept_own, new_own, other, out_k, out_v):
    for core in range(2):

        @pl.when(core_of(pos) == core)
        def _():
            for slot_out, at, part, start in (
                (0, core, kept_own, 0),
                (0, 1 - core, other, 0),
                (1, core, new_own, 0),
                (1, 1 - core, other, KVW),
            ):
                for g in range(LOCAL_KV):
                    to = slice(at * KW + g * DH, at * KW + (g + 1) * DH)
                    mid = start + (2 * g + 1) * DH
                    out_k[slot_out, :, to] = part[:, mid - DH : mid]
                    out_v[slot_out, :, to] = part[:, mid : mid + DH]


def place_kv(where, kept_own, new, other):
    return pl.pallas_call(
        place_kv_kernel,
        grid_spec=pltpu.PrefetchScalarGridSpec(
            num_scalar_prefetch=2,
            grid=(1,),
            in_specs=[
                pl.BlockSpec((TOK, KVW), lambda i, p, s: (0, 0)),
                pl.BlockSpec((TOK, KVW), lambda i, p, s: (0, 2 * QW // KVW)),
                pl.BlockSpec((TOK, 2 * KVW), lambda i, p, s: (0, 0)),
            ],
            out_specs=[pl.BlockSpec((2, TOK, 2 * KW), lambda i, p, s: (0, 0, 0))] * 2,
        ),
        out_shape=[jax.ShapeDtypeStruct((2, TOK, 2 * KW), BF)] * 2,
        cost_estimate=pl.CostEstimate(flops=0, bytes_accessed=2 << 20, transcendentals=0),
        compiler_params=pltpu.CompilerParams(vmem_limit_bytes=SMALL_LIMIT),
        name="place_kv",
    )(*where, kept_own, new, other)


def core_swap(x):
    return lax.ppermute(x, "seq", [(i, i ^ 1) for i in range(2 * CHIPS)])


def up(x, d):
    pairs = [(2 * z + c, 2 * (z + d) + c) for z in range(CHIPS - d) for c in range(2)]
    return lax.ppermute(x, "seq", pairs)


def down(x, d):
    pairs = [(2 * (z + d) + c, 2 * z + c) for z in range(CHIPS - d) for c in range(2)]
    return lax.ppermute(x, "seq", pairs)


def trade(swap_mask, handed, sends):
    replicas = lax.axis_size("dp")

    def branch(mask, handed, sends):
        sums = [down(x, d + 1) for d, x in enumerate(sends)]
        return lax.ppermute(handed, "dp", [(r, r ^ mask) for r in range(replicas)]), sums

    branches = [functools.partial(branch, mask) for mask in range(1, replicas)]
    return lax.switch(swap_mask[0] - 1, branches, handed, sends)


def per_device(queries, key_rows, value_rows, cotangent, episodes, send_slot, swap_mask):
    tied = lax.optimization_barrier
    where = (lax.axis_index("seq").reshape(1).astype(jnp.int32), send_slot)
    got = core_swap(pack_kv(where, key_rows, value_rows, episodes))
    chunk_h, chunk_k = make_chunks(where, key_rows, value_rows, episodes, got)
    chunks_h = [chunk_h] + [up(chunk_h, d) for d in range(1, CHIPS)]
    *chunks_h, chunk_k, queries, cotangent = tied((*chunks_h, chunk_k, queries, cotangent))
    q_other = core_swap(pack_q(where, queries, cotangent))
    chunks_k = [chunk_k] + [up(chunk_k, d) for d in range(1, CHIPS)]

    gq_own, gq_other, *parts = attention(
        where, 0, queries, cotangent, q_other, chunks_h, chunks_h
    )
    sums = [parts[0]] + [down(parts[d], d) for d in range(1, CHIPS)]
    gq_got = core_swap(gq_other)
    *chunks_k, gq_own = tied((*chunks_k, gq_own))
    kept_own, kept_other, *parts = attention(
        where, 1, queries, cotangent, q_other, chunks_k, chunks_h
    )
    *sums, gq_own, gq_got, kept_own = tied((*sums, gq_own, gq_got, kept_own))
    new, sums = trade(swap_mask, hand_over(sums, gq_own, gq_got), parts[1:])
    kv_own, kv_other = keep([parts[0]] + sums, new)
    kept_other, kv_other = core_swap(kept_other), core_swap(kv_other)
    grad_queries = place_q(where, kept_own, kept_other, new)
    grad_keys, grad_values = place_kv(where, kv_own, new, kv_other)
    return grad_queries, grad_keys, grad_values


def solution(mesh):
    spec = P("dp", "seq", None)
    return jax.shard_map(
        per_device,
        mesh=mesh,
        in_specs=(spec, spec, spec, spec, P("dp", "seq"), P("dp"), P()),
        out_specs=(spec, spec, spec),
        check_vma=False,
    )
```

```python
import functools
import math

import jax
import jax.numpy as jnp
from jax import lax
from jax.experimental import pallas as pl
from jax.experimental.pallas import tpu as pltpu
from jax.sharding import PartitionSpec as P

H = 40
KVH = 8
DH = 128
GROUPS = H // KVH
LOCAL_KV = KVH // 2
CHIPS = 4
TOK = 64
CHUNK = 2 * TOK
KEYS = CHIPS * CHUNK
QW = H * DH // 2
KW = LOCAL_KV * DH
KVW = 2 * KW
ROWS_Q = GROUPS * CHUNK
SCALE = 1.0 / math.sqrt(DH)
SCALE2 = SCALE * math.log2(math.e)
BF = jnp.bfloat16
F32 = jnp.float32
VMEM_LIMIT = 16 * 1024 * 1024
SMALL_LIMIT = 8 * 1024 * 1024


def interleave(out, rows, k, v):
    for g in range(LOCAL_KV):
        out[rows, 2 * g * DH : (2 * g + 1) * DH] = k[:, g * DH : (g + 1) * DH]
        out[rows, (2 * g + 1) * DH : (2 * g + 2) * DH] = v[:, g * DH : (g + 1) * DH]


def core_of(pos):
    return pos[0] & 1


def span_of(slot, i):
    return slot[0] ^ i


def id_tile(ids, slot, i):
    e = jnp.where(span_of(slot, i) == 0, ids[0:1, :], ids[1:2, :]).astype(F32)
    return jnp.broadcast_to(jnp.concatenate([e, e], axis=1), (16, DH))


def pack_kv_kernel(pos, slot, k, v, ids, out):
    for i in range(2):
        span = span_of(slot, i)
        interleave(out.at[i], slice(0, TOK), k.at[span], v.at[span])
        out[i, TOK : TOK + 16, 0:DH] = id_tile(ids, slot, i).astype(BF)


def pack_kv(where, key_rows, value_rows, episodes):
    return pl.pallas_call(
        pack_kv_kernel,
        grid_spec=pltpu.PrefetchScalarGridSpec(
            num_scalar_prefetch=2,
            grid=(1,),
            in_specs=[
                pl.BlockSpec((2, TOK, KW), lambda i, p, s: (0, 0, 1 - core_of(p))),
                pl.BlockSpec((2, TOK, KW), lambda i, p, s: (0, 0, 1 - core_of(p))),
                pl.BlockSpec((2, TOK), lambda i, p, s: (0, 0)),
            ],
            out_specs=pl.BlockSpec((2, TOK + 16, KVW), lambda i, p, s: (0, 0, 0)),
        ),
        out_shape=jax.ShapeDtypeStruct((2, TOK + 16, KVW), BF),
        cost_estimate=pl.CostEstimate(flops=0, bytes_accessed=1 << 20, transcendentals=0),
        compiler_params=pltpu.CompilerParams(vmem_limit_bytes=SMALL_LIMIT),
        name="pack_kv",
    )(*where, key_rows, value_rows, episodes)


def pack_q_kernel(pos, slot, q, c, out):
    out[0, 0] = q[0]
    out[0, 1] = c[0]


def pack_q(where, queries, cotangent):
    column = lambda i, p, s: (span_of(s, i), 0, 1 - core_of(p))
    return pl.pallas_call(
        pack_q_kernel,
        grid_spec=pltpu.PrefetchScalarGridSpec(
            num_scalar_prefetch=2,
            grid=(2,),
            in_specs=[pl.BlockSpec((1, TOK, QW), column)] * 2,
            out_specs=pl.BlockSpec((1, 2, TOK, QW), lambda i, p, s: (i, 0, 0, 0)),
        ),
        out_shape=jax.ShapeDtypeStruct((2, 2, TOK, QW), BF),
        cost_estimate=pl.CostEstimate(flops=0, bytes_accessed=3 << 20, transcendentals=0),
        compiler_params=pltpu.CompilerParams(vmem_limit_bytes=SMALL_LIMIT),
        name="pack_q",
    )(*where, queries, cotangent)


def chunks_kernel(pos, slot, k, v, ids, got, out_h, out_k):
    first = lax.broadcasted_iota(jnp.int32, (16, DH), 1) < TOK
    for i, out in enumerate((out_h, out_k)):
        span = span_of(slot, i)
        interleave(out, slice(0, TOK), k.at[span], v.at[span])
        out[TOK:CHUNK, :] = got[i, :TOK, :]
        theirs = got[i, TOK : TOK + 16, 0:DH].astype(F32)
        both = jnp.where(first, id_tile(ids, slot, i), theirs).astype(BF)
        out_h[CHUNK : CHUNK + 16, i * DH : (i + 1) * DH] = both


def make_chunks(where, key_rows, value_rows, episodes, got):
    own = pl.BlockSpec((2, TOK, KW), lambda i, p, s: (0, 0, core_of(p)))
    return pl.pallas_call(
        chunks_kernel,
        grid_spec=pltpu.PrefetchScalarGridSpec(
            num_scalar_prefetch=2,
            grid=(1,),
            in_specs=[
                own,
                own,
                pl.BlockSpec((2, TOK), lambda i, p, s: (0, 0)),
                pl.BlockSpec((2, TOK + 16, KVW), lambda i, p, s: (0, 0, 0)),
            ],
            out_specs=[
                pl.BlockSpec((CHUNK + 16, KVW), lambda i, p, s: (0, 0)),
                pl.BlockSpec((CHUNK, KVW), lambda i, p, s: (0, 0)),
            ],
        ),
        out_shape=[
            jax.ShapeDtypeStruct((CHUNK + 16, KVW), BF),
            jax.ShapeDtypeStruct((CHUNK, KVW), BF),
        ],
        cost_estimate=pl.CostEstimate(flops=0, bytes_accessed=2 << 20, transcendentals=0),
        compiler_params=pltpu.CompilerParams(vmem_limit_bytes=SMALL_LIMIT),
        name="make_chunks",
    )(*where, key_rows, value_rows, episodes, got)


def attention_kernel(
    pos, slot, qo, co, qx, k0, k1, k2, k3, i0, i1, i2, i3,
    gqo, gqx, p0, p1, p2, p3, bias, st, dt, pt, ds,
):
    chip = pos[0] >> 1
    core = core_of(pos)

    @pl.when(pl.program_id(0) == 0)
    def _():
        rows = lax.broadcasted_iota(jnp.int32, (CHUNK, CHUNK), 0)
        lanes = lax.broadcasted_iota(jnp.int32, (CHUNK, CHUNK), 1)
        query_pos = chip * CHUNK + ((lanes + core * TOK) & (CHUNK - 1))
        query_id = jnp.broadcast_to(i0[0:1, :].astype(F32), (CHUNK, CHUNK))
        for d, ids in enumerate((i0, i1, i2, i3)):
            key_pos = ((chip - d) & (CHIPS - 1)) * CHUNK + ((rows + core * TOK) & (CHUNK - 1))
            key_id = jnp.broadcast_to(ids[0:1, :].astype(F32), (CHUNK, CHUNK)).T
            allowed = (key_id == query_id) & (key_pos <= query_pos)
            bias[d * CHUNK : (d + 1) * CHUNK, :] = jnp.where(allowed, 0.0, -1e30).astype(F32)

    kv = [k[0:CHUNK, :] for k in (k0, k1, k2, k3)]
    keys = jnp.concatenate([x[:, :DH] for x in kv], axis=0)
    values = jnp.concatenate([x[:, DH:] for x in kv], axis=0)

    def heads(own, other):
        parts = []
        for h in range(GROUPS):
            parts.append(own[:, h * DH : (h + 1) * DH])
            parts.append(other[:, h * DH : (h + 1) * DH])
        return jnp.concatenate(parts, axis=0)

    queries = heads(qo[0], qx[0, 0])
    cots = heads(co[0], qx[0, 1])
    last = (((1,), (1,)), ((), ()))
    st[...] = lax.dot_general(keys, queries, last, preferred_element_type=F32)
    dt[...] = lax.dot_general(values, cots, last, preferred_element_type=F32)
    for h in range(GROUPS):
        cut = slice(h * CHUNK, (h + 1) * CHUNK)
        s = st[:, cut] * SCALE2 + bias[...]
        top = jnp.max(s, axis=0, keepdims=True)
        e = jnp.exp2(s - top)
        probs = e * (1.0 / jnp.sum(e, axis=0, keepdims=True))
        dprobs = dt[:, cut]
        delta = jnp.sum(probs * dprobs, axis=0, keepdims=True)
        pt[:, cut] = probs.astype(BF)
        ds[:, cut] = (probs * (dprobs - delta)).astype(BF)
    grad_k = jnp.dot(ds[...], queries, preferred_element_type=F32) * SCALE
    grad_v = jnp.dot(pt[...], cots, preferred_element_type=F32)
    for d, p in enumerate((p0, p1, p2, p3)):
        cut = slice(d * CHUNK, (d + 1) * CHUNK)
        p[:, :DH] = grad_k[cut].astype(p.dtype)
        p[:, DH:] = grad_v[cut].astype(p.dtype)
    gq_t = jnp.dot(keys.T, ds[...], preferred_element_type=F32) * SCALE
    for h in range(GROUPS):
        gq = gq_t[:, h * CHUNK : (h + 1) * CHUNK].T.astype(BF)
        gqo[:, h * DH : (h + 1) * DH] = gq[:TOK]
        gqx[:, h * DH : (h + 1) * DH] = gq[TOK:]


def attention(where, which, queries, cotangent, q_other, chunks, id_chunks):
    own = pl.BlockSpec((1, TOK, GROUPS * DH), lambda g, p, s: (span_of(s, which), 0, core_of(p) * LOCAL_KV + g))
    other = pl.BlockSpec((1, 2, TOK, GROUPS * DH), lambda g, p, s: (which, 0, 0, g))
    chunk = pl.BlockSpec((CHUNK, 2 * DH), lambda g, p, s: (0, g))
    ids = pl.BlockSpec((16, DH), lambda g, p, s: (CHUNK // 16, which))
    out_q = pl.BlockSpec((TOK, GROUPS * DH), lambda g, p, s: (0, g))
    return pl.pallas_call(
        attention_kernel,
        grid_spec=pltpu.PrefetchScalarGridSpec(
            num_scalar_prefetch=2,
            grid=(LOCAL_KV,),
            in_specs=[own, own, other] + [chunk] * 4 + [ids] * 4,
            out_specs=[out_q, out_q] + [chunk] * 4,
            scratch_shapes=[
                pltpu.VMEM((KEYS, CHUNK), F32),
                pltpu.VMEM((KEYS, ROWS_Q), F32),
                pltpu.VMEM((KEYS, ROWS_Q), F32),
                pltpu.VMEM((KEYS, ROWS_Q), BF),
                pltpu.VMEM((KEYS, ROWS_Q), BF),
            ],
        ),
        out_shape=[jax.ShapeDtypeStruct((TOK, QW), BF)] * 2
        + [jax.ShapeDtypeStruct((CHUNK, KVW), F32)]
        + [jax.ShapeDtypeStruct((CHUNK, KVW), BF)] * 3,
        compiler_params=pltpu.CompilerParams(
            dimension_semantics=("arbitrary",), vmem_limit_bytes=VMEM_LIMIT
        ),
        cost_estimate=pl.CostEstimate(
            flops=10 * KEYS * ROWS_Q * DH * LOCAL_KV,
            bytes_accessed=5 << 20,
            transcendentals=KEYS * ROWS_Q * LOCAL_KV,
        ),
        name="attention",
    )(*where, queries, cotangent, q_other, *chunks, *id_chunks)


def total_of(p0, r1, r2, r3):
    total = (p0[...] + r1[...].astype(F32)) + (r2[...].astype(F32) + r3[...].astype(F32))
    return total.astype(BF)


def hand_over_kernel(p0, r1, r2, r3, gq_own, gq_got, out):
    total = total_of(p0, r1, r2, r3)
    out[:, 0:QW] = gq_own[...]
    out[:, QW : 2 * QW] = gq_got[...]
    out[:, 2 * QW : 2 * QW + KVW] = total[:TOK]
    out[:, 2 * QW + KVW :] = total[TOK:]


def hand_over(parts, gq_own, gq_got):
    return pl.pallas_call(
        hand_over_kernel,
        out_shape=jax.ShapeDtypeStruct((TOK, 2 * QW + 2 * KVW), BF),
        compiler_params=pltpu.CompilerParams(vmem_limit_bytes=SMALL_LIMIT),
        cost_estimate=pl.CostEstimate(flops=0, bytes_accessed=4 << 20, transcendentals=0),
        name="hand_over",
    )(*parts, gq_own, gq_got)


def keep_kernel(p0, r1, r2, r3, new, own, swap):
    total = total_of(p0, r1, r2, r3)
    own[...] = total[:TOK]
    swap[:, :KVW] = total[TOK:]
    swap[:, KVW:] = new[...]


def keep(parts, new):
    whole = lambda shape: pl.BlockSpec(shape, lambda i: (0, 0))
    return pl.pallas_call(
        keep_kernel,
        grid=(1,),
        in_specs=[whole((CHUNK, KVW))] * 4
        + [pl.BlockSpec((TOK, KVW), lambda i: (0, 2 * QW // KVW + 1))],
        out_specs=[whole((TOK, KVW)), whole((TOK, 2 * KVW))],
        out_shape=[
            jax.ShapeDtypeStruct((TOK, KVW), BF),
            jax.ShapeDtypeStruct((TOK, 2 * KVW), BF),
        ],
        compiler_params=pltpu.CompilerParams(vmem_limit_bytes=SMALL_LIMIT),
        cost_estimate=pl.CostEstimate(flops=0, bytes_accessed=2 << 20, transcendentals=0),
        name="keep",
    )(*parts, new)


def place_q_kernel(pos, slot, kept_own, kept_other, new, out):
    for core in range(2):

        @pl.when(core_of(pos) == core)
        def _():
            a = slice(core * QW, (core + 1) * QW)
            b = slice((1 - core) * QW, (2 - core) * QW)
            out[0, :, a] = kept_own[...]
            out[0, :, b] = kept_other[...]
            out[1, :, a] = new[:, :QW]
            out[1, :, b] = new[:, QW:]


def place_q(where, kept_own, kept_other, new):
    return pl.pallas_call(
        place_q_kernel,
        grid_spec=pltpu.PrefetchScalarGridSpec(
            num_scalar_prefetch=2,
            grid=(1,),
            in_specs=[pl.BlockSpec((TOK, QW), lambda i, p, s: (0, 0))] * 2
            + [pl.BlockSpec((TOK, 2 * QW), lambda i, p, s: (0, 0))],
            out_specs=pl.BlockSpec((2, TOK, 2 * QW), lambda i, p, s: (0, 0, 0)),
        ),
        out_shape=jax.ShapeDtypeStruct((2, TOK, 2 * QW), BF),
        cost_estimate=pl.CostEstimate(flops=0, bytes_accessed=3 << 20, transcendentals=0),
        compiler_params=pltpu.CompilerParams(vmem_limit_bytes=SMALL_LIMIT),
        name="place_q",
    )(*where, kept_own, kept_other, new)


def place_kv_kernel(pos, slot, kept_own, new_own, other, out_k, out_v):
    for core in range(2):

        @pl.when(core_of(pos) == core)
        def _():
            for slot_out, at, part, start in (
                (0, core, kept_own, 0),
                (0, 1 - core, other, 0),
                (1, core, new_own, 0),
                (1, 1 - core, other, KVW),
            ):
                for g in range(LOCAL_KV):
                    to = slice(at * KW + g * DH, at * KW + (g + 1) * DH)
                    mid = start + (2 * g + 1) * DH
                    out_k[slot_out, :, to] = part[:, mid - DH : mid]
                    out_v[slot_out, :, to] = part[:, mid : mid + DH]


def place_kv(where, kept_own, new, other):
    return pl.pallas_call(
        place_kv_kernel,
        grid_spec=pltpu.PrefetchScalarGridSpec(
            num_scalar_prefetch=2,
            grid=(1,),
            in_specs=[
                pl.BlockSpec((TOK, KVW), lambda i, p, s: (0, 0)),
                pl.BlockSpec((TOK, KVW), lambda i, p, s: (0, 2 * QW // KVW)),
                pl.BlockSpec((TOK, 2 * KVW), lambda i, p, s: (0, 0)),
            ],
            out_specs=[pl.BlockSpec((2, TOK, 2 * KW), lambda i, p, s: (0, 0, 0))] * 2,
        ),
        out_shape=[jax.ShapeDtypeStruct((2, TOK, 2 * KW), BF)] * 2,
        cost_estimate=pl.CostEstimate(flops=0, bytes_accessed=2 << 20, transcendentals=0),
        compiler_params=pltpu.CompilerParams(vmem_limit_bytes=SMALL_LIMIT),
        name="place_kv",
    )(*where, kept_own, new, other)


def core_swap(x):
    return lax.ppermute(x, "seq", [(i, i ^ 1) for i in range(2 * CHIPS)])


def ring(x, d):
    n = 2 * CHIPS
    return lax.ppermute(x, "seq", [(i, (i + 2 * d) % n) for i in range(n)])


def trade(swap_mask, handed, sends):
    replicas = lax.axis_size("dp")

    def branch(mask, handed, sends):
        sums = [ring(x, -d - 1) for d, x in enumerate(sends)]
        return lax.ppermute(handed, "dp", [(r, r ^ mask) for r in range(replicas)]), sums

    branches = [functools.partial(branch, mask) for mask in range(1, replicas)]
    return lax.switch(swap_mask[0] - 1, branches, handed, sends)


def per_device(queries, key_rows, value_rows, cotangent, episodes, send_slot, swap_mask):
    tied = lax.optimization_barrier
    where = (lax.axis_index("seq").reshape(1).astype(jnp.int32), send_slot)
    got = core_swap(pack_kv(where, key_rows, value_rows, episodes))
    chunk_h, chunk_k = make_chunks(where, key_rows, value_rows, episodes, got)
    chunks_h = [chunk_h] + [ring(chunk_h, d) for d in range(1, CHIPS)]
    *chunks_h, chunk_k, queries, cotangent = tied((*chunks_h, chunk_k, queries, cotangent))
    q_other = core_swap(pack_q(where, queries, cotangent))
    chunks_k = [chunk_k] + [ring(chunk_k, d) for d in range(1, CHIPS)]

    gq_own, gq_other, *parts = attention(
        where, 0, queries, cotangent, q_other, chunks_h, chunks_h
    )
    sums = [parts[0]] + [ring(parts[d], -d) for d in range(1, CHIPS)]
    gq_got = core_swap(gq_other)
    *chunks_k, gq_own = tied((*chunks_k, gq_own))
    kept_own, kept_other, *parts = attention(
        where, 1, queries, cotangent, q_other, chunks_k, chunks_h
    )
    *sums, gq_own, gq_got, kept_own = tied((*sums, gq_own, gq_got, kept_own))
    new, sums = trade(swap_mask, hand_over(sums, gq_own, gq_got), parts[1:])
    kv_own, kv_other = keep([parts[0]] + sums, new)
    kept_other, kv_other = core_swap(kept_other), core_swap(kv_other)
    grad_queries = place_q(where, kept_own, kept_other, new)
    grad_keys, grad_values = place_kv(where, kv_own, new, kv_other)
    return grad_queries, grad_keys, grad_values


def solution(mesh):
    spec = P("dp", "seq", None)
    return jax.shard_map(
        per_device,
        mesh=mesh,
        in_specs=(spec, spec, spec, spec, P("dp", "seq"), P("dp"), P()),
        out_specs=(spec, spec, spec),
        check_vma=False,
    )
```

```python
import functools
import math

import jax
import jax.numpy as jnp
from jax import lax
from jax.experimental import pallas as pl
from jax.experimental.pallas import tpu as pltpu
from jax.sharding import PartitionSpec as P

H = 40
KVH = 8
DH = 128
GROUPS = H // KVH
LOCAL_KV = KVH // 2
CHIPS = 4
TOK = 64
CHUNK = 2 * TOK
KEYS = CHIPS * CHUNK
QW = H * DH // 2
KW = LOCAL_KV * DH
KVW = 2 * KW
ROWS_Q = GROUPS * CHUNK
SCALE = 1.0 / math.sqrt(DH)
SCALE2 = SCALE * math.log2(math.e)
BF = jnp.bfloat16
F32 = jnp.float32
VMEM_LIMIT = 16 * 1024 * 1024
ORDER = (0, 1, 3, 2)
SMALL_LIMIT = 8 * 1024 * 1024


def interleave(out, rows, k, v):
    for g in range(LOCAL_KV):
        out[rows, 2 * g * DH : (2 * g + 1) * DH] = k[:, g * DH : (g + 1) * DH]
        out[rows, (2 * g + 1) * DH : (2 * g + 2) * DH] = v[:, g * DH : (g + 1) * DH]


def core_of(pos):
    return pos[0] & 1


def span_of(slot, i):
    return slot[0] ^ i


def id_tile(ids, slot, i):
    e = jnp.where(span_of(slot, i) == 0, ids[0:1, :], ids[1:2, :]).astype(F32)
    return jnp.broadcast_to(jnp.concatenate([e, e], axis=1), (16, DH))


def pack_kv_kernel(pos, slot, k, v, ids, out):
    for i in range(2):
        span = span_of(slot, i)
        interleave(out.at[i], slice(0, TOK), k.at[span], v.at[span])
        out[i, TOK : TOK + 16, 0:DH] = id_tile(ids, slot, i).astype(BF)


def pack_kv(where, key_rows, value_rows, episodes):
    return pl.pallas_call(
        pack_kv_kernel,
        grid_spec=pltpu.PrefetchScalarGridSpec(
            num_scalar_prefetch=2,
            grid=(1,),
            in_specs=[
                pl.BlockSpec((2, TOK, KW), lambda i, p, s: (0, 0, 1 - core_of(p))),
                pl.BlockSpec((2, TOK, KW), lambda i, p, s: (0, 0, 1 - core_of(p))),
                pl.BlockSpec((2, TOK), lambda i, p, s: (0, 0)),
            ],
            out_specs=pl.BlockSpec((2, TOK + 16, KVW), lambda i, p, s: (0, 0, 0)),
        ),
        out_shape=jax.ShapeDtypeStruct((2, TOK + 16, KVW), BF),
        cost_estimate=pl.CostEstimate(flops=0, bytes_accessed=1 << 20, transcendentals=0),
        compiler_params=pltpu.CompilerParams(vmem_limit_bytes=SMALL_LIMIT),
        name="pack_kv",
    )(*where, key_rows, value_rows, episodes)


def pack_q_kernel(pos, slot, q, c, out):
    out[0, 0] = q[0]
    out[0, 1] = c[0]


def pack_q(where, queries, cotangent):
    column = lambda i, p, s: (span_of(s, i), 0, 1 - core_of(p))
    return pl.pallas_call(
        pack_q_kernel,
        grid_spec=pltpu.PrefetchScalarGridSpec(
            num_scalar_prefetch=2,
            grid=(2,),
            in_specs=[pl.BlockSpec((1, TOK, QW), column)] * 2,
            out_specs=pl.BlockSpec((1, 2, TOK, QW), lambda i, p, s: (i, 0, 0, 0)),
        ),
        out_shape=jax.ShapeDtypeStruct((2, 2, TOK, QW), BF),
        cost_estimate=pl.CostEstimate(flops=0, bytes_accessed=3 << 20, transcendentals=0),
        compiler_params=pltpu.CompilerParams(vmem_limit_bytes=SMALL_LIMIT),
        name="pack_q",
    )(*where, queries, cotangent)


def chunks_kernel(pos, slot, k, v, ids, got, top, bottom, out_k):
    first = lax.broadcasted_iota(jnp.int32, (16, DH), 1) < TOK
    for i, out in enumerate((top, out_k)):
        span = span_of(slot, i)
        interleave(out, slice(0, TOK), k.at[span], v.at[span])
        theirs = got[i, TOK : TOK + 16, 0:DH].astype(F32)
        both = jnp.where(first, id_tile(ids, slot, i), theirs).astype(BF)
        bottom[TOK : TOK + 16, i * DH : (i + 1) * DH] = both
    bottom[0:TOK, :] = got[0, :TOK, :]
    out_k[TOK:CHUNK, :] = got[1, :TOK, :]


def make_chunks(where, key_rows, value_rows, episodes, got):
    own = pl.BlockSpec((2, TOK, KW), lambda i, p, s: (0, 0, core_of(p)))
    return pl.pallas_call(
        chunks_kernel,
        grid_spec=pltpu.PrefetchScalarGridSpec(
            num_scalar_prefetch=2,
            grid=(1,),
            in_specs=[
                own,
                own,
                pl.BlockSpec((2, TOK), lambda i, p, s: (0, 0)),
                pl.BlockSpec((2, TOK + 16, KVW), lambda i, p, s: (0, 0, 0)),
            ],
            out_specs=[
                pl.BlockSpec((TOK, KVW), lambda i, p, s: (0, 0)),
                pl.BlockSpec((TOK + 16, KVW), lambda i, p, s: (0, 0)),
                pl.BlockSpec((CHUNK, KVW), lambda i, p, s: (0, 0)),
            ],
        ),
        out_shape=[
            jax.ShapeDtypeStruct((TOK, KVW), BF),
            jax.ShapeDtypeStruct((TOK + 16, KVW), BF),
            jax.ShapeDtypeStruct((CHUNK, KVW), BF),
        ],
        cost_estimate=pl.CostEstimate(flops=0, bytes_accessed=2 << 20, transcendentals=0),
        compiler_params=pltpu.CompilerParams(vmem_limit_bytes=SMALL_LIMIT),
        name="make_chunks",
    )(*where, key_rows, value_rows, episodes, got)


def attention_kernel(pos, slot, qo, co, qx, *refs):
    pieces = refs[:-15]
    i0, i1, i2, i3, gqo, gqx, p0, p1, p2, p3, bias, st, dt, pt, ds = refs[-15:]
    chip = pos[0] >> 1
    core = core_of(pos)

    @pl.when(pl.program_id(0) == 0)
    def _():
        rows = lax.broadcasted_iota(jnp.int32, (CHUNK, CHUNK), 0)
        lanes = lax.broadcasted_iota(jnp.int32, (CHUNK, CHUNK), 1)
        query_pos = chip * CHUNK + ((lanes + core * TOK) & (CHUNK - 1))
        query_id = jnp.broadcast_to(i0[0:1, :].astype(F32), (CHUNK, CHUNK))
        for at, ids in enumerate((i0, i1, i2, i3)):
            d = ORDER[at]
            key_pos = ((chip - d) & (CHIPS - 1)) * CHUNK + ((rows + core * TOK) & (CHUNK - 1))
            key_id = jnp.broadcast_to(ids[0:1, :].astype(F32), (CHUNK, CHUNK)).T
            allowed = (key_id == query_id) & (key_pos <= query_pos)
            bias[at * CHUNK : (at + 1) * CHUNK, :] = jnp.where(allowed, 0.0, -1e30).astype(F32)

    kv = [piece[...] for piece in pieces]
    keys = jnp.concatenate([x[:, :DH] for x in kv], axis=0)
    values = jnp.concatenate([x[:, DH:] for x in kv], axis=0)

    def heads(own, other):
        parts = []
        for h in range(GROUPS):
            parts.append(own[:, h * DH : (h + 1) * DH])
            parts.append(other[:, h * DH : (h + 1) * DH])
        return jnp.concatenate(parts, axis=0)

    queries = heads(qo[0], qx[0, 0])
    cots = heads(co[0], qx[0, 1])
    last = (((1,), (1,)), ((), ()))
    st[...] = lax.dot_general(keys, queries, last, preferred_element_type=F32)
    dt[...] = lax.dot_general(values, cots, last, preferred_element_type=F32)
    for h in range(GROUPS):
        cut = slice(h * CHUNK, (h + 1) * CHUNK)
        s = st[:, cut] * SCALE2 + bias[...]
        top = jnp.max(s, axis=0, keepdims=True)
        e = jnp.exp2(s - top)
        probs = e * (1.0 / jnp.sum(e, axis=0, keepdims=True))
        dprobs = dt[:, cut]
        delta = jnp.sum(probs * dprobs, axis=0, keepdims=True)
        pt[:, cut] = probs.astype(BF)
        ds[:, cut] = (probs * (dprobs - delta)).astype(BF)
    grad_k = jnp.dot(ds[...], queries, preferred_element_type=F32) * SCALE
    grad_v = jnp.dot(pt[...], cots, preferred_element_type=F32)
    for d, p in enumerate((p0, p1, p2, p3)):
        cut = slice(d * CHUNK, (d + 1) * CHUNK)
        p[:, :DH] = grad_k[cut].astype(p.dtype)
        p[:, DH:] = grad_v[cut].astype(p.dtype)
    gq_t = jnp.dot(keys.T, ds[...], preferred_element_type=F32) * SCALE
    for h in range(GROUPS):
        gq = gq_t[:, h * CHUNK : (h + 1) * CHUNK].T.astype(BF)
        gqo[:, h * DH : (h + 1) * DH] = gq[:TOK]
        gqx[:, h * DH : (h + 1) * DH] = gq[TOK:]


def attention(where, which, queries, cotangent, q_other, chunks, id_chunks):
    own = pl.BlockSpec((1, TOK, GROUPS * DH), lambda g, p, s: (span_of(s, which), 0, core_of(p) * LOCAL_KV + g))
    other = pl.BlockSpec((1, 2, TOK, GROUPS * DH), lambda g, p, s: (which, 0, 0, g))
    chunk = pl.BlockSpec((CHUNK, 2 * DH), lambda g, p, s: (0, g))
    piece = pl.BlockSpec((KEYS // len(chunks), 2 * DH), lambda g, p, s: (0, g))
    ids = pl.BlockSpec((16, DH), lambda g, p, s: (TOK // 16, which))
    out_q = pl.BlockSpec((TOK, GROUPS * DH), lambda g, p, s: (0, g))
    return pl.pallas_call(
        attention_kernel,
        grid_spec=pltpu.PrefetchScalarGridSpec(
            num_scalar_prefetch=2,
            grid=(LOCAL_KV,),
            in_specs=[own, own, other] + [piece] * len(chunks) + [ids] * 4,
            out_specs=[out_q, out_q] + [chunk] * 4,
            scratch_shapes=[
                pltpu.VMEM((KEYS, CHUNK), F32),
                pltpu.VMEM((KEYS, ROWS_Q), F32),
                pltpu.VMEM((KEYS, ROWS_Q), F32),
                pltpu.VMEM((KEYS, ROWS_Q), BF),
                pltpu.VMEM((KEYS, ROWS_Q), BF),
            ],
        ),
        out_shape=[jax.ShapeDtypeStruct((TOK, QW), BF)] * 2
        + [jax.ShapeDtypeStruct((CHUNK, KVW), F32)]
        + [jax.ShapeDtypeStruct((CHUNK, KVW), BF)] * 3,
        compiler_params=pltpu.CompilerParams(
            dimension_semantics=("arbitrary",), vmem_limit_bytes=VMEM_LIMIT
        ),
        cost_estimate=pl.CostEstimate(
            flops=10 * KEYS * ROWS_Q * DH * LOCAL_KV,
            bytes_accessed=5 << 20,
            transcendentals=KEYS * ROWS_Q * LOCAL_KV,
        ),
        name="attention",
    )(*where, queries, cotangent, q_other, *chunks, *id_chunks)


def total_of(p0, r1, r2, r3):
    total = (p0[...] + r1[...].astype(F32)) + (r2[...].astype(F32) + r3[...].astype(F32))
    return total.astype(BF)


def hand_over_kernel(p0, r1, r2, r3, gq_own, gq_got, out):
    total = total_of(p0, r1, r2, r3)
    out[:, 0:QW] = gq_own[...]
    out[:, QW : 2 * QW] = gq_got[...]
    out[:, 2 * QW : 2 * QW + KVW] = total[:TOK]
    out[:, 2 * QW + KVW :] = total[TOK:]


def hand_over(parts, gq_own, gq_got):
    return pl.pallas_call(
        hand_over_kernel,
        out_shape=jax.ShapeDtypeStruct((TOK, 2 * QW + 2 * KVW), BF),
        compiler_params=pltpu.CompilerParams(vmem_limit_bytes=SMALL_LIMIT),
        cost_estimate=pl.CostEstimate(flops=0, bytes_accessed=4 << 20, transcendentals=0),
        name="hand_over",
    )(*parts, gq_own, gq_got)


def keep_kernel(p0, r1, r2, r3, own, other):
    total = total_of(p0, r1, r2, r3)
    own[...] = total[:TOK]
    other[...] = total[TOK:]


def keep(parts):
    return pl.pallas_call(
        keep_kernel,
        out_shape=[jax.ShapeDtypeStruct((TOK, KVW), BF)] * 2,
        compiler_params=pltpu.CompilerParams(vmem_limit_bytes=SMALL_LIMIT),
        cost_estimate=pl.CostEstimate(flops=0, bytes_accessed=2 << 20, transcendentals=0),
        name="keep",
    )(*parts)


def place_q_kernel(pos, slot, kept_own, kept_other, new, out):
    for core in range(2):

        @pl.when(core_of(pos) == core)
        def _():
            a = slice(core * QW, (core + 1) * QW)
            b = slice((1 - core) * QW, (2 - core) * QW)
            out[0, :, a] = kept_own[...]
            out[0, :, b] = kept_other[...]
            out[1, :, a] = new[:, :QW]
            out[1, :, b] = new[:, QW:]


def place_q(where, kept_own, kept_other, new):
    return pl.pallas_call(
        place_q_kernel,
        grid_spec=pltpu.PrefetchScalarGridSpec(
            num_scalar_prefetch=2,
            grid=(1,),
            in_specs=[pl.BlockSpec((TOK, QW), lambda i, p, s: (0, 0))] * 2
            + [pl.BlockSpec((TOK, 2 * QW), lambda i, p, s: (0, 0))],
            out_specs=pl.BlockSpec((2, TOK, 2 * QW), lambda i, p, s: (0, 0, 0)),
        ),
        out_shape=jax.ShapeDtypeStruct((2, TOK, 2 * QW), BF),
        cost_estimate=pl.CostEstimate(flops=0, bytes_accessed=3 << 20, transcendentals=0),
        compiler_params=pltpu.CompilerParams(vmem_limit_bytes=SMALL_LIMIT),
        name="place_q",
    )(*where, kept_own, kept_other, new)


def place_kv_kernel(pos, slot, kept_own, new_own, kept_other, new_other, out_k, out_v):
    for core in range(2):

        @pl.when(core_of(pos) == core)
        def _():
            for slot_out, at, part in (
                (0, core, kept_own),
                (0, 1 - core, kept_other),
                (1, core, new_own),
                (1, 1 - core, new_other),
            ):
                for g in range(LOCAL_KV):
                    to = slice(at * KW + g * DH, at * KW + (g + 1) * DH)
                    mid = (2 * g + 1) * DH
                    out_k[slot_out, :, to] = part[:, mid - DH : mid]
                    out_v[slot_out, :, to] = part[:, mid : mid + DH]


def place_kv(where, kept_own, new, kept_other, new_other):
    return pl.pallas_call(
        place_kv_kernel,
        grid_spec=pltpu.PrefetchScalarGridSpec(
            num_scalar_prefetch=2,
            grid=(1,),
            in_specs=[
                pl.BlockSpec((TOK, KVW), lambda i, p, s: (0, 0)),
                pl.BlockSpec((TOK, KVW), lambda i, p, s: (0, 2 * QW // KVW)),
                pl.BlockSpec((TOK, KVW), lambda i, p, s: (0, 0)),
                pl.BlockSpec((TOK, KVW), lambda i, p, s: (0, 0)),
            ],
            out_specs=[pl.BlockSpec((2, TOK, 2 * KW), lambda i, p, s: (0, 0, 0))] * 2,
        ),
        out_shape=[jax.ShapeDtypeStruct((2, TOK, 2 * KW), BF)] * 2,
        cost_estimate=pl.CostEstimate(flops=0, bytes_accessed=2 << 20, transcendentals=0),
        compiler_params=pltpu.CompilerParams(vmem_limit_bytes=SMALL_LIMIT),
        name="place_kv",
    )(*where, kept_own, new, kept_other, new_other)


def core_swap(x):
    return lax.ppermute(x, "seq", [(i, i ^ 1) for i in range(2 * CHIPS)])


def ring(x, d):
    n = 2 * CHIPS
    return lax.ppermute(x, "seq", [(i, (i + 2 * d) % n) for i in range(n)])


def trade(swap_mask, handed, parts):
    replicas = lax.axis_size("dp")

    def branch(mask, handed, parts):
        sums = [ring(x, -d) for x, d in zip(parts[1:], ORDER[1:])]
        new = lax.ppermute(handed, "dp", [(r, r ^ mask) for r in range(replicas)])
        return new, keep([parts[0]] + sums)

    branches = [functools.partial(branch, mask) for mask in range(1, replicas)]
    return lax.switch(swap_mask[0] - 1, branches, handed, parts)


def per_device(queries, key_rows, value_rows, cotangent, episodes, send_slot, swap_mask):
    tied = lax.optimization_barrier
    where = (lax.axis_index("seq").reshape(1).astype(jnp.int32), send_slot)
    got = core_swap(pack_kv(where, key_rows, value_rows, episodes))
    top, bottom, chunk_k = make_chunks(where, key_rows, value_rows, episodes, got)
    top_1, bottom_3, bottom_1, top_3 = ring(top, 1), ring(bottom, 3), ring(bottom, 1), ring(top, 3)
    top_2, bottom_2 = ring(top_1, 1), ring(bottom_3, 3)
    pieces = (top, bottom, top_1, bottom_1, top_3, bottom_3, top_2, bottom_2)
    *pieces, chunk_k, queries, cotangent = tied((*pieces, chunk_k, queries, cotangent))
    q_other = core_swap(pack_q(where, queries, cotangent))
    chunks_k = [chunk_k] + [ring(chunk_k, d) for d in ORDER[1:]]

    gq_own, gq_other, *parts = attention(
        where, 0, queries, cotangent, q_other, pieces, pieces[1::2]
    )
    sums = [parts[0]] + [ring(x, -d) for x, d in zip(parts[1:], ORDER[1:])]
    gq_got = core_swap(gq_other)
    *chunks_k, gq_own = tied((*chunks_k, gq_own))
    kept_own, kept_other, *parts = attention(
        where, 1, queries, cotangent, q_other, chunks_k, pieces[1::2]
    )
    *sums, gq_own, gq_got, kept_own = tied((*sums, gq_own, gq_got, kept_own))
    new, (kv_own, kv_other) = trade(swap_mask, hand_over(sums, gq_own, gq_got), parts)
    kept_other, kv_other = core_swap(kept_other), core_swap(kv_other)
    kv_new = core_swap(new[:, 2 * QW + KVW :])
    grad_queries = place_q(where, kept_own, kept_other, new)
    grad_keys, grad_values = place_kv(where, kv_own, new, kv_other, kv_new)
    return grad_queries, grad_keys, grad_values


def solution(mesh):
    spec = P("dp", "seq", None)
    return jax.shard_map(
        per_device,
        mesh=mesh,
        in_specs=(spec, spec, spec, spec, P("dp", "seq"), P("dp"), P()),
        out_specs=(spec, spec, spec),
        check_vma=False,
    )
```

```python
import functools
import math

import jax
import jax.numpy as jnp
from jax import lax
from jax.experimental import pallas as pl
from jax.experimental.pallas import tpu as pltpu
from jax.sharding import PartitionSpec as P

H = 40
KVH = 8
DH = 128
GROUPS = H // KVH
LOCAL_KV = KVH // 2
CHIPS = 4
TOK = 64
CHUNK = 2 * TOK
KEYS = CHIPS * CHUNK
QW = H * DH // 2
KW = LOCAL_KV * DH
KVW = 2 * KW
ROWS_Q = GROUPS * CHUNK
PAIR = 2
SCALE = 1.0 / math.sqrt(DH)
SCALE2 = SCALE * math.log2(math.e)
BF = jnp.bfloat16
F32 = jnp.float32
VMEM_LIMIT = 24 * 1024 * 1024
ORDER = (0, 1, 3, 2)
SMALL_LIMIT = 8 * 1024 * 1024


def interleave(out, rows, k, v):
    for g in range(LOCAL_KV):
        out[rows, 2 * g * DH : (2 * g + 1) * DH] = k[:, g * DH : (g + 1) * DH]
        out[rows, (2 * g + 1) * DH : (2 * g + 2) * DH] = v[:, g * DH : (g + 1) * DH]


def core_of(pos):
    return pos[0] & 1


def span_of(slot, i):
    return slot[0] ^ i


def id_tile(ids, slot, i):
    e = jnp.where(span_of(slot, i) == 0, ids[0:1, :], ids[1:2, :]).astype(F32)
    return jnp.broadcast_to(jnp.concatenate([e, e], axis=1), (16, DH))


def pack_kv_kernel(pos, slot, k, v, ids, out):
    for i in range(2):
        span = span_of(slot, i)
        interleave(out.at[i], slice(0, TOK), k.at[span], v.at[span])
        out[i, TOK : TOK + 16, 0:DH] = id_tile(ids, slot, i).astype(BF)


def pack_kv(where, key_rows, value_rows, episodes):
    return pl.pallas_call(
        pack_kv_kernel,
        grid_spec=pltpu.PrefetchScalarGridSpec(
            num_scalar_prefetch=2,
            grid=(1,),
            in_specs=[
                pl.BlockSpec((2, TOK, KW), lambda i, p, s: (0, 0, 1 - core_of(p))),
                pl.BlockSpec((2, TOK, KW), lambda i, p, s: (0, 0, 1 - core_of(p))),
                pl.BlockSpec((2, TOK), lambda i, p, s: (0, 0)),
            ],
            out_specs=pl.BlockSpec((2, TOK + 16, KVW), lambda i, p, s: (0, 0, 0)),
        ),
        out_shape=jax.ShapeDtypeStruct((2, TOK + 16, KVW), BF),
        cost_estimate=pl.CostEstimate(flops=0, bytes_accessed=1 << 20, transcendentals=0),
        compiler_params=pltpu.CompilerParams(vmem_limit_bytes=SMALL_LIMIT),
        name="pack_kv",
    )(*where, key_rows, value_rows, episodes)


def pack_q_kernel(pos, slot, q, c, out):
    out[0, 0] = q[0]
    out[0, 1] = c[0]


def pack_q(where, queries, cotangent):
    column = lambda i, p, s: (span_of(s, i), 0, 1 - core_of(p))
    return pl.pallas_call(
        pack_q_kernel,
        grid_spec=pltpu.PrefetchScalarGridSpec(
            num_scalar_prefetch=2,
            grid=(2,),
            in_specs=[pl.BlockSpec((1, TOK, QW), column)] * 2,
            out_specs=pl.BlockSpec((1, 2, TOK, QW), lambda i, p, s: (i, 0, 0, 0)),
        ),
        out_shape=jax.ShapeDtypeStruct((2, 2, TOK, QW), BF),
        cost_estimate=pl.CostEstimate(flops=0, bytes_accessed=3 << 20, transcendentals=0),
        compiler_params=pltpu.CompilerParams(vmem_limit_bytes=SMALL_LIMIT),
        name="pack_q",
    )(*where, queries, cotangent)


def chunks_kernel(pos, slot, k, v, ids, got, top, bottom, out_k):
    first = lax.broadcasted_iota(jnp.int32, (16, DH), 1) < TOK
    for i, out in enumerate((top, out_k)):
        span = span_of(slot, i)
        interleave(out, slice(0, TOK), k.at[span], v.at[span])
        theirs = got[i, TOK : TOK + 16, 0:DH].astype(F32)
        both = jnp.where(first, id_tile(ids, slot, i), theirs).astype(BF)
        bottom[TOK : TOK + 16, i * DH : (i + 1) * DH] = both
    bottom[0:TOK, :] = got[0, :TOK, :]
    out_k[TOK:CHUNK, :] = got[1, :TOK, :]


def make_chunks(where, key_rows, value_rows, episodes, got):
    own = pl.BlockSpec((2, TOK, KW), lambda i, p, s: (0, 0, core_of(p)))
    return pl.pallas_call(
        chunks_kernel,
        grid_spec=pltpu.PrefetchScalarGridSpec(
            num_scalar_prefetch=2,
            grid=(1,),
            in_specs=[
                own,
                own,
                pl.BlockSpec((2, TOK), lambda i, p, s: (0, 0)),
                pl.BlockSpec((2, TOK + 16, KVW), lambda i, p, s: (0, 0, 0)),
            ],
            out_specs=[
                pl.BlockSpec((TOK, KVW), lambda i, p, s: (0, 0)),
                pl.BlockSpec((TOK + 16, KVW), lambda i, p, s: (0, 0)),
                pl.BlockSpec((CHUNK, KVW), lambda i, p, s: (0, 0)),
            ],
        ),
        out_shape=[
            jax.ShapeDtypeStruct((TOK, KVW), BF),
            jax.ShapeDtypeStruct((TOK + 16, KVW), BF),
            jax.ShapeDtypeStruct((CHUNK, KVW), BF),
        ],
        cost_estimate=pl.CostEstimate(flops=0, bytes_accessed=2 << 20, transcendentals=0),
        compiler_params=pltpu.CompilerParams(vmem_limit_bytes=SMALL_LIMIT),
        name="make_chunks",
    )(*where, key_rows, value_rows, episodes, got)


def attention_kernel(pos, slot, qo, co, qx, *refs):
    pieces = refs[:-15]
    i0, i1, i2, i3, gqo, gqx, p0, p1, p2, p3, bias, st, dt, pt, ds = refs[-15:]
    chip = pos[0] >> 1
    core = core_of(pos)

    @pl.when(pl.program_id(0) == 0)
    def _():
        rows = lax.broadcasted_iota(jnp.int32, (CHUNK, CHUNK), 0)
        lanes = lax.broadcasted_iota(jnp.int32, (CHUNK, CHUNK), 1)
        query_pos = chip * CHUNK + ((lanes + core * TOK) & (CHUNK - 1))
        query_id = jnp.broadcast_to(i0[0:1, :].astype(F32), (CHUNK, CHUNK))
        for at, ids in enumerate((i0, i1, i2, i3)):
            d = ORDER[at]
            key_pos = ((chip - d) & (CHIPS - 1)) * CHUNK + ((rows + core * TOK) & (CHUNK - 1))
            key_id = jnp.broadcast_to(ids[0:1, :].astype(F32), (CHUNK, CHUNK)).T
            allowed = (key_id == query_id) & (key_pos <= query_pos)
            bias[at * CHUNK : (at + 1) * CHUNK, :] = jnp.where(allowed, 0.0, -1e30).astype(F32)

    for u in range(PAIR):
        wide, narrow = u * GROUPS * DH, u * 2 * DH
        cols = slice(wide, wide + GROUPS * DH)
        kv = [piece[:, narrow : narrow + 2 * DH] for piece in pieces]
        keys = jnp.concatenate([x[:, :DH] for x in kv], axis=0)
        values = jnp.concatenate([x[:, DH:] for x in kv], axis=0)

        def heads(own, other):
            parts = []
            for h in range(GROUPS):
                parts.append(own[:, h * DH : (h + 1) * DH])
                parts.append(other[:, h * DH : (h + 1) * DH])
            return jnp.concatenate(parts, axis=0)

        queries = heads(qo[0, :, cols], qx[0, 0, :, cols])
        cots = heads(co[0, :, cols], qx[0, 1, :, cols])
        last = (((1,), (1,)), ((), ()))
        st[u] = lax.dot_general(keys, queries, last, preferred_element_type=F32)
        dt[u] = lax.dot_general(values, cots, last, preferred_element_type=F32)
        for h in range(GROUPS):
            cut = slice(h * CHUNK, (h + 1) * CHUNK)
            s = st[u, :, cut] * SCALE2 + bias[...]
            top = jnp.max(s, axis=0, keepdims=True)
            e = jnp.exp2(s - top)
            probs = e * (1.0 / jnp.sum(e, axis=0, keepdims=True))
            dprobs = dt[u, :, cut]
            delta = jnp.sum(probs * dprobs, axis=0, keepdims=True)
            pt[u, :, cut] = probs.astype(BF)
            ds[u, :, cut] = (probs * (dprobs - delta)).astype(BF)
        grad_k = jnp.dot(ds[u], queries, preferred_element_type=F32) * SCALE
        grad_v = jnp.dot(pt[u], cots, preferred_element_type=F32)
        for d, p in enumerate((p0, p1, p2, p3)):
            cut = slice(d * CHUNK, (d + 1) * CHUNK)
            p[:, narrow : narrow + DH] = grad_k[cut].astype(p.dtype)
            p[:, narrow + DH : narrow + 2 * DH] = grad_v[cut].astype(p.dtype)
        gq_t = jnp.dot(keys.T, ds[u], preferred_element_type=F32) * SCALE
        for h in range(GROUPS):
            gq = gq_t[:, h * CHUNK : (h + 1) * CHUNK].T.astype(BF)
            gqo[:, wide + h * DH : wide + (h + 1) * DH] = gq[:TOK]
            gqx[:, wide + h * DH : wide + (h + 1) * DH] = gq[TOK:]


def attention(where, which, queries, cotangent, q_other, chunks, id_chunks):
    own = pl.BlockSpec((1, TOK, PAIR * GROUPS * DH), lambda g, p, s: (span_of(s, which), 0, core_of(p) * (LOCAL_KV // PAIR) + g))
    other = pl.BlockSpec((1, 2, TOK, PAIR * GROUPS * DH), lambda g, p, s: (which, 0, 0, g))
    chunk = pl.BlockSpec((CHUNK, PAIR * 2 * DH), lambda g, p, s: (0, g))
    piece = pl.BlockSpec((KEYS // len(chunks), PAIR * 2 * DH), lambda g, p, s: (0, g))
    ids = pl.BlockSpec((16, DH), lambda g, p, s: (TOK // 16, which))
    out_q = pl.BlockSpec((TOK, PAIR * GROUPS * DH), lambda g, p, s: (0, g))
    return pl.pallas_call(
        attention_kernel,
        grid_spec=pltpu.PrefetchScalarGridSpec(
            num_scalar_prefetch=2,
            grid=(LOCAL_KV // PAIR,),
            in_specs=[own, own, other] + [piece] * len(chunks) + [ids] * 4,
            out_specs=[out_q, out_q] + [chunk] * 4,
            scratch_shapes=[
                pltpu.VMEM((KEYS, CHUNK), F32),
                pltpu.VMEM((PAIR, KEYS, ROWS_Q), F32),
                pltpu.VMEM((PAIR, KEYS, ROWS_Q), F32),
                pltpu.VMEM((PAIR, KEYS, ROWS_Q), BF),
                pltpu.VMEM((PAIR, KEYS, ROWS_Q), BF),
            ],
        ),
        out_shape=[jax.ShapeDtypeStruct((TOK, QW), BF)] * 2
        + [jax.ShapeDtypeStruct((CHUNK, KVW), F32)]
        + [jax.ShapeDtypeStruct((CHUNK, KVW), BF)] * 3,
        compiler_params=pltpu.CompilerParams(
            dimension_semantics=("arbitrary",), vmem_limit_bytes=VMEM_LIMIT
        ),
        cost_estimate=pl.CostEstimate(
            flops=10 * KEYS * ROWS_Q * DH * LOCAL_KV,
            bytes_accessed=5 << 20,
            transcendentals=KEYS * ROWS_Q * LOCAL_KV,
        ),
        name="attention",
    )(*where, queries, cotangent, q_other, *chunks, *id_chunks)


def total_of(p0, r1, r2, r3):
    total = (p0[...] + r1[...].astype(F32)) + (r2[...].astype(F32) + r3[...].astype(F32))
    return total.astype(BF)


def hand_over_kernel(p0, r1, r2, r3, gq_own, gq_got, out):
    total = total_of(p0, r1, r2, r3)
    out[:, 0:QW] = gq_own[...]
    out[:, QW : 2 * QW] = gq_got[...]
    out[:, 2 * QW : 2 * QW + KVW] = total[:TOK]
    out[:, 2 * QW + KVW :] = total[TOK:]


def hand_over(parts, gq_own, gq_got):
    return pl.pallas_call(
        hand_over_kernel,
        out_shape=jax.ShapeDtypeStruct((TOK, 2 * QW + 2 * KVW), BF),
        compiler_params=pltpu.CompilerParams(vmem_limit_bytes=SMALL_LIMIT),
        cost_estimate=pl.CostEstimate(flops=0, bytes_accessed=4 << 20, transcendentals=0),
        name="hand_over",
    )(*parts, gq_own, gq_got)


def keep_kernel(p0, r1, r2, r3, own, other):
    total = total_of(p0, r1, r2, r3)
    own[...] = total[:TOK]
    other[...] = total[TOK:]


def keep(parts):
    return pl.pallas_call(
        keep_kernel,
        out_shape=[jax.ShapeDtypeStruct((TOK, KVW), BF)] * 2,
        compiler_params=pltpu.CompilerParams(vmem_limit_bytes=SMALL_LIMIT),
        cost_estimate=pl.CostEstimate(flops=0, bytes_accessed=2 << 20, transcendentals=0),
        name="keep",
    )(*parts)


def place_q_kernel(pos, slot, kept_own, kept_other, new, out):
    for core in range(2):

        @pl.when(core_of(pos) == core)
        def _():
            a = slice(core * QW, (core + 1) * QW)
            b = slice((1 - core) * QW, (2 - core) * QW)
            out[0, :, a] = kept_own[...]
            out[0, :, b] = kept_other[...]
            out[1, :, a] = new[:, :QW]
            out[1, :, b] = new[:, QW:]


def place_q(where, kept_own, kept_other, new):
    return pl.pallas_call(
        place_q_kernel,
        grid_spec=pltpu.PrefetchScalarGridSpec(
            num_scalar_prefetch=2,
            grid=(1,),
            in_specs=[pl.BlockSpec((TOK, QW), lambda i, p, s: (0, 0))] * 2
            + [pl.BlockSpec((TOK, 2 * QW), lambda i, p, s: (0, 0))],
            out_specs=pl.BlockSpec((2, TOK, 2 * QW), lambda i, p, s: (0, 0, 0)),
        ),
        out_shape=jax.ShapeDtypeStruct((2, TOK, 2 * QW), BF),
        cost_estimate=pl.CostEstimate(flops=0, bytes_accessed=3 << 20, transcendentals=0),
        compiler_params=pltpu.CompilerParams(vmem_limit_bytes=SMALL_LIMIT),
        name="place_q",
    )(*where, kept_own, kept_other, new)


def place_kv_kernel(pos, slot, kept_own, new_own, kept_other, new_other, out_k, out_v):
    for core in range(2):

        @pl.when(core_of(pos) == core)
        def _():
            for slot_out, at, part in (
                (0, core, kept_own),
                (0, 1 - core, kept_other),
                (1, core, new_own),
                (1, 1 - core, new_other),
            ):
                for g in range(LOCAL_KV):
                    to = slice(at * KW + g * DH, at * KW + (g + 1) * DH)
                    mid = (2 * g + 1) * DH
                    out_k[slot_out, :, to] = part[:, mid - DH : mid]
                    out_v[slot_out, :, to] = part[:, mid : mid + DH]


def place_kv(where, kept_own, new, kept_other, new_other):
    return pl.pallas_call(
        place_kv_kernel,
        grid_spec=pltpu.PrefetchScalarGridSpec(
            num_scalar_prefetch=2,
            grid=(1,),
            in_specs=[
                pl.BlockSpec((TOK, KVW), lambda i, p, s: (0, 0)),
                pl.BlockSpec((TOK, KVW), lambda i, p, s: (0, 2 * QW // KVW)),
                pl.BlockSpec((TOK, KVW), lambda i, p, s: (0, 0)),
                pl.BlockSpec((TOK, KVW), lambda i, p, s: (0, 0)),
            ],
            out_specs=[pl.BlockSpec((2, TOK, 2 * KW), lambda i, p, s: (0, 0, 0))] * 2,
        ),
        out_shape=[jax.ShapeDtypeStruct((2, TOK, 2 * KW), BF)] * 2,
        cost_estimate=pl.CostEstimate(flops=0, bytes_accessed=2 << 20, transcendentals=0),
        compiler_params=pltpu.CompilerParams(vmem_limit_bytes=SMALL_LIMIT),
        name="place_kv",
    )(*where, kept_own, new, kept_other, new_other)


def core_swap(x):
    return lax.ppermute(x, "seq", [(i, i ^ 1) for i in range(2 * CHIPS)])


def ring(x, d):
    n = 2 * CHIPS
    return lax.ppermute(x, "seq", [(i, (i + 2 * d) % n) for i in range(n)])


def trade(swap_mask, handed, parts):
    replicas = lax.axis_size("dp")

    def branch(mask, handed, parts):
        sums = [ring(x, -d) for x, d in zip(parts[1:], ORDER[1:])]
        new = lax.ppermute(handed, "dp", [(r, r ^ mask) for r in range(replicas)])
        return new, keep([parts[0]] + sums)

    branches = [functools.partial(branch, mask) for mask in range(1, replicas)]
    return lax.switch(swap_mask[0] - 1, branches, handed, parts)


def per_device(queries, key_rows, value_rows, cotangent, episodes, send_slot, swap_mask):
    tied = lax.optimization_barrier
    where = (lax.axis_index("seq").reshape(1).astype(jnp.int32), send_slot)
    got = core_swap(pack_kv(where, key_rows, value_rows, episodes))
    top, bottom, chunk_k = make_chunks(where, key_rows, value_rows, episodes, got)
    top_1, bottom_3, bottom_1, top_3 = ring(top, 1), ring(bottom, 3), ring(bottom, 1), ring(top, 3)
    top_2, bottom_2 = ring(top_1, 1), ring(bottom_3, 3)
    pieces = (top, bottom, top_1, bottom_1, top_3, bottom_3, top_2, bottom_2)
    *pieces, chunk_k, queries, cotangent = tied((*pieces, chunk_k, queries, cotangent))
    q_other = core_swap(pack_q(where, queries, cotangent))
    chunks_k = [chunk_k] + [ring(chunk_k, d) for d in ORDER[1:]]

    gq_own, gq_other, *parts = attention(
        where, 0, queries, cotangent, q_other, pieces, pieces[1::2]
    )
    sums = [parts[0]] + [ring(x, -d) for x, d in zip(parts[1:], ORDER[1:])]
    gq_got = core_swap(gq_other)
    *chunks_k, gq_own = tied((*chunks_k, gq_own))
    kept_own, kept_other, *parts = attention(
        where, 1, queries, cotangent, q_other, chunks_k, pieces[1::2]
    )
    *sums, gq_own, gq_got, kept_own = tied((*sums, gq_own, gq_got, kept_own))
    new, (kv_own, kv_other) = trade(swap_mask, hand_over(sums, gq_own, gq_got), parts)
    kept_other, kv_other = core_swap(kept_other), core_swap(kv_other)
    kv_new = core_swap(new[:, 2 * QW + KVW :])
    grad_queries = place_q(where, kept_own, kept_other, new)
    grad_keys, grad_values = place_kv(where, kv_own, new, kv_other, kv_new)
    return grad_queries, grad_keys, grad_values


def solution(mesh):
    spec = P("dp", "seq", None)
    return jax.shard_map(
        per_device,
        mesh=mesh,
        in_specs=(spec, spec, spec, spec, P("dp", "seq"), P("dp"), P()),
        out_specs=(spec, spec, spec),
        check_vma=False,
    )
```
